256 devices in a mesh: req: 32 (over x, z), tp: 8 (over y, core).
Axes of the slice: x: 4, y: 4, z: 8, core: 2. Of those that a mesh axis runs over, the one named last changes fastest.
Arguments:
- queries: bfloat16 [4, 1024, 8192], P(None, 'req', 'tp'), may hold values from -8 to 8
- new_kv: bfloat16 [4, 1024, 2, 1024], P(None, 'req', None, 'tp'), may hold values from -8 to 8
- prefill_page_pool: bfloat16 [8192, 2, 16, 1024], P('req', None, None, 'tp'), may hold values from -6 to 6
- page_table: int32 [1024, 8], P('req'), may hold values from 0 to 255, as said below
- prompt_len: int32 [1024], P('req'), may hold values from 1 to 128
- dest_device: int32 [1024], P('req'), may hold values from 0 to 31, as said below
- ssm_state: float32 [1024, 16, 16384], P('req', None, 'tp'), may hold values from -4 to 4
- conv_state: bfloat16 [1024, 3, 16384], P('req', None, 'tp'), may hold values from -6 to 6
- mamba_x: bfloat16 [4, 1024, 16384], P(None, 'req', 'tp'), may hold values from -6 to 6
- mamba_z: bfloat16 [4, 1024, 16384], P(None, 'req', 'tp'), may hold values from -6 to 6
- conv_weight: float32 [4, 16384], P(None, 'tp'), may hold values from -3 to 3
- conv_bias: float32 [16384], P('tp'), may hold values from -0.5 to 0.5
- x_proj: bfloat16 [16384, 544], P('tp'), may hold values from -0.046875 to 0.046875
- dt_gain: float32 [512], replicated, may hold values from 0.25 to 1.75
- dt_proj: bfloat16 [512, 16384], P(None, 'tp'), may hold values from -0.25 to 0.25
- dt_bias: float32 [16384], P('tp'), may hold values from -3 to 0
- a_log: float32 [16, 16384], P(None, 'tp'), may hold values from -1 to 2.8
- skip_d: float32 [16384], P('tp'), may hold values from 0.5 to 1.5
Outputs:
- attn_out: bfloat16 [4, 1024, 8192], P(None, 'req', 'tp')
- mamba_out: bfloat16 [4, 1024, 16384], P(None, 'req', 'tp')
The draws below stay inside these ranges and needn't reach their ends.
Inputs may be any that keep to these rules, and one draw needn't show every extreme that they name: `dest_device`: each prefill device hands exactly 1 of its requests to every decode device. `page_table`: the entries of one prefill device's rows are distinct pages of its own pool; only the first ceil(prompt_len / 16) of a row hold the request's tokens.
All inputs are finite; a program needn't handle non-finite values.
Results may differ from the reference program's by a relative error of at most 0.01.
Values may be sent and summed in bfloat16 or wider, within the bound.
No kernel may reach another device: no remote copies, remote signals or barrier semaphores. Data moves between devices by JAX's collectives and lax.ppermute only.
A program may use at most 128 MiB of HBM per device.

```python
import math
import jax
import jax.numpy as jnp
from jax import lax

QUERY_HEADS = 64
KEY_VALUE_HEADS = 8
HEAD_SIZE = 128
CH = 16384
STATE = 16
DT_RANK = 512
CONV = 4
DECODE_STEPS = 4
PAGE_TOKENS = 16
LMAX = 128
REQ_DEV = 32
PAGE_LIST_MAX = 8
RPP = 1
REQUEST_TOTAL = 1024
N_REQ = 32
N_TP = 8


def shared_routes(key):
    device_keys = jax.random.split(key, N_REQ)

    def one_device(device_key):
        return jax.random.permutation(device_key, REQ_DEV)
    shuffled = jax.vmap(one_device)(device_keys)
    return (shuffled // RPP).reshape(REQUEST_TOTAL).astype(jnp.int32)


def draw_dest_device(key, part):
    return shared_routes(key)


def draw_prompt_len(key, part):
    destinations = shared_routes(key)
    key = jax.random.fold_in(key, 11)
    first, second, third_part = jax.random.split(key, 3)
    heavy_phase = jax.random.randint(first, (), 0, 8)
    heavy = destinations % 8 == heavy_phase
    caps = jnp.where(heavy, LMAX, max(LMAX // 4, 1))
    raw_draws = jax.random.randint(second, (REQUEST_TOTAL,), 0, 1 << 20)
    lengths = 1 + raw_draws % caps
    priority = jax.random.permutation(third_part, REQUEST_TOTAL)
    chosen = jnp.argmax(jnp.where(heavy, priority, -1))
    lengths = lengths.at[chosen].set(LMAX)
    return lengths.astype(jnp.int32)


def draw_page_table(key, part):
    key = jax.random.fold_in(key, 23)
    device_keys = jax.random.split(key, N_REQ)

    def one_device(device_key):
        return jax.random.permutation(device_key, REQ_DEV * PAGE_LIST_MAX)
    return jax.vmap(one_device)(device_keys).reshape(REQUEST_TOTAL, PAGE_LIST_MAX).astype(jnp.int32)


def draw_queries(key, part):
    key = jax.random.fold_in(key, 31)
    simple_value = jnp.clip(jax.random.normal(key, (DECODE_STEPS, REQUEST_TOTAL, QUERY_HEADS, HEAD_SIZE), jnp.float32), -8.0, 8.0)
    return simple_value.reshape(DECODE_STEPS, REQUEST_TOTAL, QUERY_HEADS * HEAD_SIZE).astype(jnp.bfloat16)


def draw_new_kv(key, part):
    key = jax.random.fold_in(key, 37)
    simple_value = jnp.clip(jax.random.normal(key, (DECODE_STEPS, REQUEST_TOTAL, 2, KEY_VALUE_HEADS, HEAD_SIZE), jnp.float32), -8.0, 8.0)
    return simple_value.reshape(DECODE_STEPS, REQUEST_TOTAL, 2, KEY_VALUE_HEADS * HEAD_SIZE).astype(jnp.bfloat16)


def shard_levels(own_key, dims, pieces, smallest, largest):
    gain, own = 1.0, jax.random.fold_in(own_key, 6)
    for axis_at, blocks in pieces:
        draws = jnp.exp(jax.random.uniform(jax.random.fold_in(own, axis_at), (blocks,), jnp.float32, smallest / len(pieces), largest / len(pieces)))
        gain = gain * jnp.repeat(draws, dims[axis_at] // blocks).reshape([-1 if axis == axis_at else 1 for axis in range(len(dims))])
    return gain


def gaussian(stream_key, extent, width, most, pieces=(), kind=jnp.bfloat16):
    factor_of = shard_levels(stream_key, extent, pieces, -0.22, 0.18) if pieces else 1.0
    drawn = jax.random.normal(stream_key, extent, jnp.float32) * width * factor_of
    return jnp.minimum(jnp.maximum(drawn, -most), most).astype(kind)


def setup_inputs(seed: int = 0) -> dict:
    seeds = jax.random.split(jax.random.key(seed), 19)
    return {
        "queries": draw_queries(jax.random.fold_in(seeds[18], 71), 0),
        "new_kv": draw_new_kv(jax.random.fold_in(seeds[18], 71), 0),
        "prefill_page_pool": gaussian(seeds[2], (REQUEST_TOTAL * PAGE_LIST_MAX, 2, PAGE_TOKENS, KEY_VALUE_HEADS * HEAD_SIZE), 1.0, 6.0, ((0, 32), (3, 8))),
        "page_table": draw_page_table(jax.random.fold_in(seeds[18], 71), 0),
        "prompt_len": draw_prompt_len(jax.random.fold_in(seeds[18], 71), 0),
        "dest_device": draw_dest_device(jax.random.fold_in(seeds[18], 71), 0),
        "ssm_state": gaussian(seeds[6], (REQUEST_TOTAL, STATE, CH), 0.5, 4.0, ((0, 32), (2, 8)), jnp.float32),
        "conv_state": gaussian(seeds[7], (REQUEST_TOTAL, CONV - 1, CH), 1.0, 6.0, ((0, 32), (2, 8))),
        "mamba_x": gaussian(seeds[8], (DECODE_STEPS, REQUEST_TOTAL, CH), 1.0, 6.0, ((1, 32), (2, 8))),
        "mamba_z": gaussian(seeds[9], (DECODE_STEPS, REQUEST_TOTAL, CH), 1.0, 6.0, ((1, 32), (2, 8))),
        "conv_weight": gaussian(seeds[10], (CONV, CH), CONV ** -0.5, 3.0, ((1, 8),), jnp.float32),
        "conv_bias": jnp.clip(jax.random.uniform(seeds[11], (CH,), jnp.float32, -0.5, 0.5) * shard_levels(seeds[11], (CH,), ((0, 8),), -0.4, 0.0), -0.5, 0.5),
        "x_proj": gaussian(seeds[12], (CH, DT_RANK + 2 * STATE), CH ** -0.5, 0.046875, ((0, 8),)),
        "dt_gain": jnp.clip(1.0 + 0.15 * jax.random.normal(seeds[13], (DT_RANK,), jnp.float32), 0.25, 1.75),
        "dt_proj": gaussian(seeds[14], (DT_RANK, CH), DT_RANK ** -0.5, 0.25, ((1, 8),)),
        "dt_bias": jnp.clip(-3.0 + 3.0 * jax.random.uniform(seeds[15], (CH,), jnp.float32) ** shard_levels(seeds[15], (CH,), ((0, 8),), -0.2, 0.2), -3.0, 0.0),
        "a_log": jnp.clip(-1.0 + 3.8 * jax.random.uniform(seeds[16], (STATE, CH), jnp.float32) ** shard_levels(seeds[16], (STATE, CH), ((1, 8),), -0.2, 0.2), -1.0, 2.8),
        "skip_d": jnp.clip(0.5 + 1.0 * jax.random.uniform(seeds[17], (CH,), jnp.float32) ** shard_levels(seeds[17], (CH,), ((0, 8),), -0.2, 0.2), 0.5, 1.5),
    }


EPSILON = 1e-06
HIGHEST = lax.Precision.HIGHEST

def source_rows(dest_device):
    targets = dest_device.reshape(N_REQ, REQ_DEV)
    earlier = jnp.arange(REQ_DEV)[None, :] < jnp.arange(REQ_DEV)[:, None]
    matching = targets[:, :, None] == targets[:, None, :]
    ranking = lax.optimization_barrier(jnp.sum(jnp.where(matching & earlier[None], 1, 0), axis=2)).astype(jnp.int32)
    devices = jnp.arange(N_REQ, dtype=jnp.int32)[:, None]
    slot_index = (targets * REQ_DEV + devices * RPP + ranking).reshape(REQUEST_TOTAL).astype(jnp.int32)
    everything = jnp.arange(REQUEST_TOTAL, dtype=jnp.int32)
    return jnp.zeros((REQUEST_TOTAL,), jnp.int32).at[slot_index].set(everything)

def attention(queries, new_kv, prefill_page_pool, page_table, prompt_len, source_row):
    group_width = QUERY_HEADS // KEY_VALUE_HEADS
    cache_len = PAGE_LIST_MAX * PAGE_TOKENS
    page_ids = (source_row // REQ_DEV * (REQ_DEV * PAGE_LIST_MAX))[:, None] + page_table[source_row]
    lengths = prompt_len[source_row]
    key_valid = jnp.arange(cache_len)[None, :] < lengths[:, None]
    causal = jnp.arange(DECODE_STEPS)[None, :] <= jnp.arange(DECODE_STEPS)[:, None]
    score_scale = 1.0 / math.sqrt(HEAD_SIZE)
    all_queries = queries.reshape(DECODE_STEPS, REQUEST_TOTAL, QUERY_HEADS, HEAD_SIZE)

    def single_head(head_index):
        first_col = head_index * HEAD_SIZE
        head_cache = lax.dynamic_slice_in_dim(prefill_page_pool, first_col, HEAD_SIZE, 3)
        picked = head_cache[page_ids]
        cache_keys = picked[:, :, 0].reshape(REQUEST_TOTAL, cache_len, HEAD_SIZE).astype(jnp.float32)
        cache_values = picked[:, :, 1].reshape(REQUEST_TOTAL, cache_len, HEAD_SIZE).astype(jnp.float32)
        fresh_kv = lax.dynamic_slice_in_dim(new_kv, first_col, HEAD_SIZE, 3).astype(jnp.float32)
        head_query = lax.dynamic_slice_in_dim(all_queries, head_index * group_width, group_width, 2).astype(jnp.float32)
        cached_scores = jnp.einsum('trgd,rsd->trgs', head_query, cache_keys, precision=HIGHEST) * score_scale
        cached_scores = jnp.where(key_valid[None, :, None, :], cached_scores, -jnp.inf)
        recent_scores = jnp.einsum('trgd,urd->trgu', head_query, fresh_kv[:, :, 0], precision=HIGHEST) * score_scale
        recent_scores = jnp.where(causal[:, None, None, :], recent_scores, -jnp.inf)
        scores = jnp.concatenate([cached_scores, recent_scores], axis=3)
        row_max = lax.optimization_barrier(jnp.max(scores, axis=3, keepdims=True))
        weights = jnp.exp(scores - row_max)
        row_total = lax.optimization_barrier(jnp.sum(weights, axis=3, keepdims=True))
        weighted = jnp.einsum('trgs,rsd->trgd', weights[..., :cache_len], cache_values, precision=HIGHEST)
        weighted = weighted + jnp.einsum('trgu,urd->trgd', weights[..., cache_len:], fresh_kv[:, :, 1], precision=HIGHEST)
        return weighted / row_total
    each_head_value = lax.map(single_head, jnp.arange(KEY_VALUE_HEADS, dtype=jnp.int32))
    return jnp.transpose(each_head_value, (1, 2, 0, 3, 4)).reshape(DECODE_STEPS, REQUEST_TOTAL, QUERY_HEADS * HEAD_SIZE).astype(jnp.bfloat16)

def mamba_layer(ssm_state, conv_state, mamba_x, mamba_z, conv_weight, conv_bias, x_proj, dt_gain, dt_proj, dt_bias, a_log, skip_d, source_row):
    window = jnp.concatenate([jnp.transpose(conv_state[source_row], (1, 0, 2)).astype(jnp.float32), mamba_x.astype(jnp.float32)], axis=0)
    convolved = conv_bias + sum((conv_weight[offset] * window[offset:offset + DECODE_STEPS] for offset in range(CONV)))
    conv_out = jax.nn.silu(convolved).astype(jnp.bfloat16)
    proj = jnp.dot(conv_out.reshape(DECODE_STEPS * REQUEST_TOTAL, CH), x_proj, preferred_element_type=jnp.float32).reshape(DECODE_STEPS, REQUEST_TOTAL, DT_RANK + 2 * STATE)
    dt_low = proj[..., :DT_RANK]
    b_coef = proj[..., DT_RANK:DT_RANK + STATE]
    c_coef = proj[..., DT_RANK + STATE:]
    normed = (dt_low * lax.rsqrt(lax.optimization_barrier(jnp.mean(dt_low * dt_low, axis=-1, keepdims=True)) + EPSILON) * dt_gain).astype(jnp.bfloat16)
    flat_normed = normed.reshape(DECODE_STEPS * REQUEST_TOTAL, DT_RANK)
    block_width = CH // N_TP

    def one_block(block_index):
        first_col = block_index * block_width
        proj_block = lax.dynamic_slice_in_dim(dt_proj, first_col, block_width, 1)
        bias_block = lax.dynamic_slice_in_dim(dt_bias, first_col, block_width, 0)
        step_rate = jax.nn.softplus(jnp.dot(flat_normed, proj_block, preferred_element_type=jnp.float32).reshape(DECODE_STEPS, REQUEST_TOTAL, block_width) + bias_block)
        decay_log = -jnp.exp(lax.dynamic_slice_in_dim(a_log, first_col, block_width, 1))
        inputs = lax.dynamic_slice_in_dim(conv_out, first_col, block_width, 2).astype(jnp.float32)
        gate_values = jax.nn.silu(lax.dynamic_slice_in_dim(mamba_z, first_col, block_width, 2).astype(jnp.float32))
        skip_block = lax.dynamic_slice_in_dim(skip_d, first_col, block_width, 0)
        hidden_state = lax.dynamic_slice_in_dim(ssm_state, first_col, block_width, 2)[source_row]
        outputs = []
        for moment in range(DECODE_STEPS):
            hidden_state = jnp.exp(step_rate[moment][:, None, :] * decay_log[None]) * hidden_state + (step_rate[moment] * inputs[moment])[:, None, :] * b_coef[moment][:, :, None]
            reading = lax.optimization_barrier(jnp.sum(c_coef[moment][:, :, None] * hidden_state, axis=1)) + skip_block * inputs[moment]
            outputs.append(reading * gate_values[moment])
        return jnp.stack(outputs)
    per_block = lax.map(one_block, jnp.arange(N_TP, dtype=jnp.int32))
    return jnp.transpose(per_block, (1, 2, 0, 3)).reshape(DECODE_STEPS, REQUEST_TOTAL, CH).astype(jnp.bfloat16)

def reference(queries, new_kv, prefill_page_pool, page_table, prompt_len, dest_device, ssm_state, conv_state, mamba_x, mamba_z, conv_weight, conv_bias, x_proj, dt_gain, dt_proj, dt_bias, a_log, skip_d):
    source_row = source_rows(dest_device)
    attn_out = attention(queries, new_kv, prefill_page_pool, page_table, prompt_len, source_row)
    mamba_out = mamba_layer(ssm_state, conv_state, mamba_x, mamba_z, conv_weight, conv_bias, x_proj, dt_gain, dt_proj, dt_bias, a_log, skip_d, source_row)
    return (attn_out, mamba_out)
```

```python
import math

import jax
import jax.numpy as jnp
from jax import lax
from jax.sharding import PartitionSpec as P

HEAD_SIZE = 128
EPSILON = 1e-06


def tp_total(partial, dt_gain, rank_width):
    half = partial.shape[0] // 2
    core = lax.axis_index("tp") % 2
    low, high = partial[:half], partial[half:]
    mine = jnp.where(core == 0, low, high)
    other = jnp.where(core == 0, high, low)
    swap = [(j, j ^ 1) for j in range(8)]
    chip_sum = mine + lax.ppermute(other, "tp", swap)
    small = chip_sum.astype(jnp.bfloat16)
    total = chip_sum
    for hop in (2, 6, 4):
        got = lax.ppermute(small, "tp", [(j, (j + hop) % 8) for j in range(8)])
        total = total + got.astype(jnp.float32)
    dt_low = total[:, :rank_width]
    normed = (
        dt_low
        * lax.rsqrt(jnp.mean(dt_low * dt_low, axis=-1, keepdims=True) + EPSILON)
        * dt_gain
    ).astype(jnp.bfloat16)
    coef = total[:, rank_width:]
    coef_high = coef.astype(jnp.bfloat16)
    coef_low = (coef - coef_high.astype(jnp.float32)).astype(jnp.bfloat16)
    packed = jnp.concatenate([normed, coef_high, coef_low], axis=1)
    theirs = lax.ppermute(packed, "tp", swap)
    first = jnp.where(core == 0, packed, theirs)
    second = jnp.where(core == 0, theirs, packed)
    both = jnp.concatenate([first, second], axis=0)
    width = coef.shape[1]
    coef = both[:, rank_width : rank_width + width].astype(jnp.float32) + both[
        :, rank_width + width :
    ].astype(jnp.float32)
    return both[:, :rank_width], coef


def per_device(
    queries,
    new_kv,
    prefill_page_pool,
    page_table,
    prompt_len,
    dest_device,
    ssm_state,
    conv_state,
    mamba_x,
    mamba_z,
    conv_weight,
    conv_bias,
    x_proj,
    dt_gain,
    dt_proj,
    dt_bias,
    a_log,
    skip_d,
):
    steps, reqs, channels = mamba_x.shape
    rank_width = dt_proj.shape[0]
    state_size = a_log.shape[0]
    heads = queries.shape[2] // HEAD_SIZE
    cache_len = page_table.shape[1] * prefill_page_pool.shape[2]
    scale = 1.0 / math.sqrt(HEAD_SIZE)
    slots = jnp.arange(reqs, dtype=jnp.int32)
    order = jnp.sum(
        jnp.where(dest_device[None, :] == slots[:, None], slots[None, :], 0), axis=1
    )
    outgoing = jnp.concatenate(
        [
            jnp.transpose(mamba_x, (1, 0, 2)),
            jnp.transpose(queries, (1, 0, 2)),
            jnp.transpose(new_kv.reshape(steps, reqs, 2 * HEAD_SIZE), (1, 0, 2)),
        ],
        axis=2,
    )
    arrived = lax.all_to_all(outgoing, "req", split_axis=0, concat_axis=0, tiled=True)
    x_rows = arrived[:, :, :channels].astype(jnp.float32)
    query = arrived[:, :, channels : channels + heads * HEAD_SIZE].reshape(
        reqs, steps, heads, HEAD_SIZE
    )
    fresh = arrived[:, :, channels + heads * HEAD_SIZE :].reshape(reqs, steps, 2, HEAD_SIZE)

    window = jnp.concatenate([conv_state[order].astype(jnp.float32), x_rows], axis=1)
    convolved = conv_bias + sum(
        conv_weight[tap] * window[:, tap : tap + steps] for tap in range(conv_weight.shape[0])
    )
    conv_out = jax.nn.silu(convolved).astype(jnp.bfloat16)
    partial = jnp.dot(
        conv_out.reshape(reqs * steps, channels), x_proj, preferred_element_type=jnp.float32
    )
    normed, coef = tp_total(partial, dt_gain, rank_width)

    picked = prefill_page_pool[page_table[order]]
    keys = picked[:, :, 0].reshape(reqs, cache_len, HEAD_SIZE)
    values = picked[:, :, 1].reshape(reqs, cache_len, HEAD_SIZE)
    valid = jnp.arange(cache_len)[None, :] < prompt_len[order][:, None]
    flat_query = query.reshape(reqs, steps * heads, HEAD_SIZE)
    old = jnp.einsum("rqd,rsd->rqs", flat_query, keys, preferred_element_type=jnp.float32) * scale
    old = jnp.where(valid[:, None, :], old, -jnp.inf)
    new = (
        jnp.einsum("rqd,rud->rqu", flat_query, fresh[:, :, 0], preferred_element_type=jnp.float32)
        * scale
    )
    causal = jnp.arange(steps)[None, :] <= (jnp.arange(steps * heads) // heads)[:, None]
    new = jnp.where(causal[None], new, -jnp.inf)
    top = jnp.maximum(jnp.max(old, axis=2), jnp.max(new, axis=2))[..., None]
    old = jnp.exp(old - top)
    new = jnp.exp(new - top)
    total = jnp.sum(old, axis=2) + jnp.sum(new, axis=2)
    weighted = jnp.einsum(
        "rqs,rsd->rqd", old.astype(jnp.bfloat16), values, preferred_element_type=jnp.float32
    ) + jnp.einsum(
        "rqu,rud->rqd",
        new.astype(jnp.bfloat16),
        fresh[:, :, 1],
        preferred_element_type=jnp.float32,
    )
    attended = (weighted / total[..., None]).astype(jnp.bfloat16)
    attended = attended.reshape(reqs, steps, heads * HEAD_SIZE)

    rate = jax.nn.softplus(
        jnp.dot(normed, dt_proj, preferred_element_type=jnp.float32) + dt_bias
    ).reshape(reqs, steps, channels)
    coef = coef.reshape(reqs, steps, 2 * state_size)
    decay = -jnp.exp(a_log)
    inputs = conv_out.astype(jnp.float32)
    hidden = ssm_state[order]
    readings = []
    for step in range(steps):
        hidden = (
            jnp.exp(rate[:, step, None, :] * decay[None]) * hidden
            + (rate[:, step] * inputs[:, step])[:, None, :] * coef[:, step, :state_size, None]
        )
        readings.append(
            jnp.sum(coef[:, step, state_size:, None] * hidden, axis=1) + skip_d * inputs[:, step]
        )
    reading = jnp.stack(readings, axis=1).astype(jnp.bfloat16)

    returning = jnp.concatenate([reading, attended], axis=2)
    back = lax.all_to_all(returning, "req", split_axis=0, concat_axis=0, tiled=True)
    back = jnp.transpose(back, (1, 0, 2))
    gate = jax.nn.silu(mamba_z.astype(jnp.float32))
    mamba_out = (back[:, :, :channels].astype(jnp.float32) * gate).astype(jnp.bfloat16)
    return back[:, :, channels:], mamba_out


def solution(mesh):
    return jax.shard_map(
        per_device,
        mesh=mesh,
        in_specs=(
            P(None, "req", "tp"),
            P(None, "req", None, "tp"),
            P("req", None, None, "tp"),
            P("req", None),
            P("req"),
            P("req"),
            P("req", None, "tp"),
            P("req", None, "tp"),
            P(None, "req", "tp"),
            P(None, "req", "tp"),
            P(None, "tp"),
            P("tp"),
            P("tp", None),
            P(),
            P(None, "tp"),
            P("tp"),
            P(None, "tp"),
            P("tp"),
        ),
        out_specs=(P(None, "req", "tp"), P(None, "req", "tp")),
        check_vma=False,
    )
```

```python
import math

import jax
import jax.numpy as jnp
from jax import lax
from jax.experimental import pallas as pl
from jax.experimental.pallas import tpu as pltpu
from jax.sharding import PartitionSpec as P

HEAD_SIZE = 128
EPSILON = 1e-06
REQS = 32
STEPS = 4
ROWS = 2 * STEPS
LANES = 128
HALF = 1024
QUARTER = 512
RANK = 512
STATE = 16
PAGES = 8
PAGE_TOKENS = 16
PROJ = RANK + 2 * STATE
SEND = HALF + QUARTER + HEAD_SIZE
BACK = HALF + QUARTER
F32 = jnp.float32
BF16 = jnp.bfloat16


def vmem():
    return pl.BlockSpec(memory_space=pltpu.VMEM)


def smem():
    return pl.BlockSpec(memory_space=pltpu.SMEM)


def params(mib):
    return pltpu.CompilerParams(vmem_limit_bytes=mib * 1024 * 1024)


def sublanes(shape):
    return lax.broadcasted_iota(jnp.int32, shape, len(shape) - 2)


def pack_kernel(x_ref, q_ref, kv_ref, out_ref, rows):
    sources = ((x_ref, HALF), (q_ref, QUARTER), (kv_ref, HEAD_SIZE))
    for step in range(STEPS):
        for group in range(0, REQS, 16):
            for half in range(2):
                first = half * STEPS + step
                places = [
                    pl.ds((group + part * 8) * ROWS + first, 8, stride=ROWS) for part in range(2)
                ]
                tile = 0
                for ref, width in sources:
                    block = ref[step, group : group + 16, half * width : (half + 1) * width]
                    block = block.astype(F32)
                    for column in range(0, width, LANES):
                        rows[tile, places[0], :] = block[0:8, column : column + LANES]
                        rows[tile, places[1], :] = block[8:16, column : column + LANES]
                        tile += 1
    for req in range(REQS):
        for tile in range(SEND // LANES):
            out_ref[req, :, tile * LANES : (tile + 1) * LANES] = rows[
                tile, req * ROWS : (req + 1) * ROWS, :
            ].astype(BF16)


def pack(mamba_x, queries, new_kv):
    return pl.pallas_call(
        pack_kernel,
        out_shape=jax.ShapeDtypeStruct((REQS, ROWS, SEND), BF16),
        in_specs=[vmem()] * 3,
        out_specs=vmem(),
        scratch_shapes=[pltpu.VMEM((SEND // LANES, REQS * ROWS, LANES), F32)],
        compiler_params=params(24),
        name="pack",
    )(mamba_x, queries, new_kv)


def halves(ref, row, width):
    low = jnp.broadcast_to(ref[row : row + 1, 0:width], (STEPS, width))
    high = jnp.broadcast_to(ref[row : row + 1, width : 2 * width], (STEPS, width))
    return jnp.concatenate([low, high], axis=0)


def conv_kernel(
    order_ref,
    core_ref,
    rows_ref,
    past_ref,
    weight_ref,
    bias_ref,
    proj_ref,
    act_ref,
    mine_ref,
    other_ref,
    taps,
    part,
):
    for tap in range(4):
        taps[tap] = halves(weight_ref, tap, HALF)
    taps[4] = halves(bias_ref, 0, HALF)
    step_of = lax.rem(sublanes((ROWS, HALF)), STEPS)
    blank = jnp.zeros((1, HALF), F32)

    def one(req):
        now = rows_ref[req, :, 0:HALF].astype(F32)
        past = past_ref[order_ref[req]].astype(F32)
        past = jnp.concatenate([blank, past[:, HALF:], blank, past[:, :HALF]], axis=0)
        total = taps[4] + taps[3] * now
        for back in range(1, 4):
            mixed = jnp.where(step_of >= STEPS - back, past, now)
            total = total + taps[3 - back] * pltpu.roll(mixed, back, 0)
        return total * jax.nn.sigmoid(total)

    def pair(index, carry):
        both = jnp.concatenate([one(2 * index), one(2 * index + 1)], axis=0)
        act_ref[pl.ds(pl.multiple_of(index * 16, 16), 16), :] = both.astype(BF16)
        return carry

    lax.fori_loop(0, REQS // 2, pair, 0)
    act = act_ref[...]
    low = jnp.dot(act, proj_ref[0:HALF, :], preferred_element_type=F32)
    high = jnp.dot(act, proj_ref[HALF : 2 * HALF, :], preferred_element_type=F32)
    upper = sublanes((ROWS, PROJ)) < STEPS
    for index in range(REQS // 2):
        even = slice(index * 16, index * 16 + 8)
        odd = slice(index * 16 + 8, index * 16 + 16)
        own = jnp.where(upper, low[even], high[odd])
        cross = jnp.where(upper, low[odd], high[even])
        part[index * 8 : index * 8 + 8, :] = own + pltpu.roll(cross, STEPS, 0)
    core = core_ref[0]
    size = REQS * STEPS // 2
    mine_ref[...] = part[pl.ds(pl.multiple_of(core * size, size), size), :]
    other_ref[...] = part[pl.ds(pl.multiple_of((1 - core) * size, size), size), :]


def convolve(order, core, arrived, conv_state, conv_weight, conv_bias, x_proj):
    half_rows = jax.ShapeDtypeStruct((REQS * STEPS // 2, PROJ), F32)
    return pl.pallas_call(
        conv_kernel,
        out_shape=(jax.ShapeDtypeStruct((REQS * ROWS, HALF), BF16), half_rows, half_rows),
        in_specs=[smem(), smem()] + [vmem()] * 5,
        out_specs=(vmem(), vmem(), vmem()),
        scratch_shapes=[
            pltpu.VMEM((5, ROWS, HALF), F32),
            pltpu.VMEM((REQS * STEPS, PROJ), F32),
        ],
        compiler_params=params(24),
        name="convolve",
    )(order, core, arrived, conv_state, conv_weight, conv_bias, x_proj)


def norm_kernel(sum_ref, one_ref, two_ref, three_ref, gain_ref, out_ref):
    total = (
        sum_ref[...]
        + one_ref[...].astype(F32)
        + two_ref[...].astype(F32)
        + three_ref[...].astype(F32)
    )
    low = total[:, :RANK]
    spread = lax.rsqrt(jnp.mean(low * low, axis=-1, keepdims=True) + EPSILON)
    out_ref[:, 0:RANK] = (low * spread * gain_ref[...]).astype(BF16)
    coef = total[:, RANK:]
    coef = jnp.concatenate([coef, jnp.zeros((coef.shape[0], LANES - 2 * STATE), F32)], axis=1)
    coef_high = coef.astype(BF16)
    out_ref[:, RANK : RANK + LANES] = coef_high
    out_ref[:, RANK + LANES :] = (coef - coef_high.astype(F32)).astype(BF16)


def normalise(chip_sum, ring, gain):
    return pl.pallas_call(
        norm_kernel,
        out_shape=jax.ShapeDtypeStruct((REQS * STEPS // 2, RANK + 2 * LANES), BF16),
        in_specs=[vmem()] * 5,
        out_specs=vmem(),
        compiler_params=params(8),
        name="normalise",
    )(chip_sum, *ring, gain)


def attend_kernel(order_ref, table_ref, length_ref, rows_ref, pool_ref, out_ref):
    scale = 1.0 / math.sqrt(HEAD_SIZE)
    wide = (4 * ROWS, 2 * LANES)
    lane = lax.broadcasted_iota(jnp.int32, wide, 1)
    step_of = lax.rem(lax.broadcasted_iota(jnp.int32, wide, 0), STEPS)
    fresh_ok = (lane >= LANES) & (lane - LANES <= step_of)
    pad = jnp.zeros((LANES - PAGE_TOKENS, HEAD_SIZE), BF16)
    blank = jnp.zeros((ROWS, HEAD_SIZE), F32)

    def one(req):
        source = order_ref[req]
        pages = [table_ref[source, page] for page in range(PAGES)]
        length = length_ref[source]
        query = rows_ref[req, :, HALF : HALF + QUARTER].astype(F32)
        query = jnp.concatenate(
            [query[:, h * HEAD_SIZE : (h + 1) * HEAD_SIZE] for h in range(4)], axis=0
        ).astype(BF16)
        fresh = rows_ref[req, :, HALF + QUARTER : SEND].astype(F32)
        fresh_keys = jnp.concatenate([fresh, blank], axis=0).astype(BF16)
        fresh_values = jnp.concatenate([pltpu.roll(fresh, STEPS, 0), blank], axis=0).astype(BF16)
        keys = jnp.concatenate([pool_ref[p, 0] for p in pages] + [fresh_keys, pad], axis=0)
        values = jnp.concatenate([pool_ref[p, 1] for p in pages] + [fresh_values, pad], axis=0)
        scores = (
            lax.dot_general(query, keys, (((1,), (1,)), ((), ())), preferred_element_type=F32)
            * scale
        )
        scores = jnp.where((lane < length) & (lane < LANES) | fresh_ok, scores, -jnp.inf)
        weights = jnp.exp(scores - jnp.max(scores, axis=1, keepdims=True))
        total = jnp.sum(weights, axis=1, keepdims=True)
        mixed = jnp.dot(weights.astype(BF16), values, preferred_element_type=F32) / total
        for h in range(4):
            out_ref[req, :, h * HEAD_SIZE : (h + 1) * HEAD_SIZE] = mixed[
                h * ROWS : (h + 1) * ROWS
            ].astype(BF16)

    def some(index, carry):
        for offset in range(4):
            one(4 * index + offset)
        return carry

    lax.fori_loop(0, REQS // 4, some, 0)


def attend(order, page_table, prompt_len, arrived, pool):
    return pl.pallas_call(
        attend_kernel,
        out_shape=jax.ShapeDtypeStruct((REQS, ROWS, QUARTER), BF16),
        in_specs=[smem()] * 3 + [vmem()] * 2,
        out_specs=vmem(),
        compiler_params=params(16),
        cost_estimate=pl.CostEstimate(
            flops=300_000_000, bytes_accessed=6_000_000, transcendentals=300_000
        ),
        name="attend",
    )(order, page_table, prompt_len, arrived, pool)


def gather_rows(parts, sub):
    four = sub < 4
    parts = [
        jnp.where(four, parts[s], parts[s + 4])
        + pltpu.roll(jnp.where(four, parts[s + 4], parts[s]), 4, 0)
        for s in range(4)
    ]
    two = lax.rem(sub, 4) < 2
    parts = [
        jnp.where(
            two,
            parts[s] + pltpu.roll(parts[s], 6, 0),
            parts[s + 2] + pltpu.roll(parts[s + 2], 2, 0),
        )
        for s in range(2)
    ]
    return jnp.where(
        lax.rem(sub, 2) < 1,
        parts[0] + pltpu.roll(parts[0], 7, 0),
        parts[1] + pltpu.roll(parts[1], 1, 0),
    )


def scan_kernel(
    order_ref,
    core_ref,
    ours_ref,
    theirs_ref,
    act_ref,
    attended_ref,
    state_ref,
    dt_proj_ref,
    dt_bias_ref,
    a_log_ref,
    skip_ref,
    out_ref,
    packed,
    rate,
    fed,
    decay,
    skip,
    coef,
):
    core = core_ref[0]
    size = REQS * STEPS // 2
    packed[pl.ds(pl.multiple_of(core * size, size), size), :] = ours_ref[...]
    packed[pl.ds(pl.multiple_of((1 - core) * size, size), size), :] = theirs_ref[...]
    skip[...] = halves(skip_ref, 0, HALF)
    decay[...] = jnp.exp(a_log_ref[...]) * (-1.0 / math.log(2.0))
    coef[...] = jnp.transpose(
        packed[:, RANK : RANK + LANES].astype(F32) + packed[:, RANK + LANES :].astype(F32)
    )
    upper = sublanes((ROWS, HALF)) < STEPS
    normed = packed[:, 0:RANK]
    low = jnp.dot(normed, dt_proj_ref[:, 0:HALF], preferred_element_type=F32)
    low = jax.nn.softplus(low + dt_bias_ref[:, 0:HALF])
    high = jnp.dot(normed, dt_proj_ref[:, HALF:], preferred_element_type=F32)
    high = jax.nn.softplus(high + dt_bias_ref[:, HALF:])
    for index in range(REQS // 2):
        rows = slice(index * 8, index * 8 + 8)
        even = jnp.where(upper, low[rows], pltpu.roll(high[rows], STEPS, 0))
        odd = jnp.where(upper, pltpu.roll(low[rows], STEPS, 0), high[rows])
        both = jnp.concatenate([even, odd], axis=0)
        span = slice(index * 16, index * 16 + 16)
        both_fed = both * act_ref[span, :].astype(F32)
        rate[2 * index] = even
        rate[2 * index + 1] = odd
        fed[2 * index] = both_fed[0:8]
        fed[2 * index + 1] = both_fed[8:16]
    sub = sublanes((ROWS, LANES))

    def one(req, act):
        source = order_ref[req]
        turned = pltpu.roll(coef[0 : 2 * STATE, :], lax.rem(LANES - STEPS * req, LANES), 1)
        into = [
            jnp.broadcast_to(turned[0:STATE, s : s + 1], (STATE, LANES)) for s in range(STEPS)
        ]
        read = [
            jnp.broadcast_to(turned[STATE : 2 * STATE, s : s + 1], (STATE, LANES))
            for s in range(STEPS)
        ]
        for tile in range(HALF // LANES):
            place = slice(tile * LANES, (tile + 1) * LANES)
            parts = []
            for half in range(2):
                columns = slice(half * HALF + tile * LANES, half * HALF + (tile + 1) * LANES)
                hidden = state_ref[source, :, columns]
                slope = decay[:, columns]
                for step in range(STEPS):
                    row = slice(half * STEPS + step, half * STEPS + step + 1)
                    hidden = (
                        jnp.exp2(jnp.broadcast_to(rate[req, row, place], (STATE, LANES)) * slope) * hidden
                        + jnp.broadcast_to(fed[req, row, place], (STATE, LANES)) * into[step]
                    )
                    seen = hidden * read[step]
                    parts.append(seen[0:8] + seen[8:16])
            summed = gather_rows(parts, sub) + skip[:, place] * act[:, place]
            out_ref[req, :, place] = summed.astype(BF16)
        out_ref[req, :, HALF:BACK] = attended_ref[req]

    def pair(index, carry):
        act = act_ref[pl.ds(pl.multiple_of(index * 16, 16), 16), :].astype(F32)
        one(2 * index, act[0:8])
        one(2 * index + 1, act[8:16])
        return carry

    lax.fori_loop(0, REQS // 2, pair, 0)


def scan(order, core, ours, theirs, act, attended, ssm_state, dt_proj, dt_bias, a_log, skip_d):
    return pl.pallas_call(
        scan_kernel,
        out_shape=jax.ShapeDtypeStruct((REQS, ROWS, BACK), BF16),
        in_specs=[smem(), smem()] + [vmem()] * 9,
        out_specs=vmem(),
        scratch_shapes=[
            pltpu.VMEM((REQS * STEPS, RANK + 2 * LANES), BF16),
            pltpu.VMEM((REQS, ROWS, HALF), F32),
            pltpu.VMEM((REQS, ROWS, HALF), F32),
            pltpu.VMEM((STATE, 2 * HALF), F32),
            pltpu.VMEM((ROWS, HALF), F32),
            pltpu.VMEM((LANES, LANES), F32),
        ],
        compiler_params=params(32),
        name="scan",
    )(order, core, ours, theirs, act, attended, ssm_state, dt_proj, dt_bias, a_log, skip_d)


def unpack_kernel(back_ref, z_ref, attn_ref, mamba_ref, rows):
    for req in range(REQS):
        for tile in range(BACK // LANES):
            rows[tile, req * ROWS : (req + 1) * ROWS, :] = back_ref[
                req, :, tile * LANES : (tile + 1) * LANES
            ].astype(F32)
    for step in range(STEPS):
        for group in range(0, REQS, 16):
            for half in range(2):
                first = half * STEPS + step
                places = [
                    pl.ds((group + part * 8) * ROWS + first, 8, stride=ROWS) for part in range(2)
                ]
                for tile in range(BACK // LANES):
                    block = jnp.concatenate([rows[tile, place, :] for place in places], axis=0)
                    if tile < HALF // LANES:
                        first_column = half * HALF + tile * LANES
                        columns = slice(first_column, first_column + LANES)
                        z = z_ref[step, group : group + 16, columns].astype(F32)
                        block = block * (z * jax.nn.sigmoid(z))
                        mamba_ref[step, group : group + 16, columns] = block.astype(BF16)
                    else:
                        first_column = half * QUARTER + tile * LANES - HALF
                        columns = slice(first_column, first_column + LANES)
                        attn_ref[step, group : group + 16, columns] = block.astype(BF16)


def unpack(back, mamba_z):
    return pl.pallas_call(
        unpack_kernel,
        out_shape=(
            jax.ShapeDtypeStruct((STEPS, REQS, 2 * QUARTER), BF16),
            jax.ShapeDtypeStruct((STEPS, REQS, 2 * HALF), BF16),
        ),
        in_specs=[vmem()] * 2,
        out_specs=(vmem(), vmem()),
        scratch_shapes=[pltpu.VMEM((BACK // LANES, REQS * ROWS, LANES), F32)],
        compiler_params=params(24),
        name="unpack",
    )(back, mamba_z)


def per_device(
    queries,
    new_kv,
    prefill_page_pool,
    page_table,
    prompt_len,
    dest_device,
    ssm_state,
    conv_state,
    mamba_x,
    mamba_z,
    conv_weight,
    conv_bias,
    x_proj,
    dt_gain,
    dt_proj,
    dt_bias,
    a_log,
    skip_d,
):
    slots = jnp.arange(REQS, dtype=jnp.int32)
    order = jnp.sum(
        jnp.where(dest_device[None, :] == slots[:, None], slots[None, :], 0), axis=1
    )
    core = (lax.axis_index("tp") % 2).astype(jnp.int32).reshape(1)
    swap = [(j, j ^ 1) for j in range(8)]

    outgoing = pack(mamba_x, queries, new_kv.reshape(STEPS, REQS, 2 * HEAD_SIZE))
    arrived = lax.all_to_all(outgoing, "req", split_axis=0, concat_axis=0, tiled=True)
    act, mine, other = convolve(
        order, core, arrived, conv_state, conv_weight, conv_bias[None], x_proj
    )
    chip_sum = mine + lax.ppermute(other, "tp", swap)
    small = chip_sum.astype(BF16)
    ring = [
        lax.ppermute(small, "tp", [(j, (j + hop) % 8) for j in range(8)]) for hop in (2, 6, 4)
    ]
    attended = attend(order, page_table, prompt_len, arrived, prefill_page_pool)
    ours = normalise(chip_sum, ring, dt_gain[None])
    theirs = lax.ppermute(ours, "tp", swap)
    returning = scan(
        order,
        core,
        ours,
        theirs,
        act,
        attended,
        ssm_state,
        dt_proj,
        dt_bias[None],
        a_log,
        skip_d[None],
    )
    back = lax.all_to_all(returning, "req", split_axis=0, concat_axis=0, tiled=True)
    return unpack(back, mamba_z)


def solution(mesh):
    return jax.shard_map(
        per_device,
        mesh=mesh,
        in_specs=(
            P(None, "req", "tp"),
            P(None, "req", None, "tp"),
            P("req", None, None, "tp"),
            P("req", None),
            P("req"),
            P("req"),
            P("req", None, "tp"),
            P("req", None, "tp"),
            P(None, "req", "tp"),
            P(None, "req", "tp"),
            P(None, "tp"),
            P("tp"),
            P("tp", None),
            P(),
            P(None, "tp"),
            P("tp"),
            P(None, "tp"),
            P("tp"),
        ),
        out_specs=(P(None, "req", "tp"), P(None, "req", "tp")),
        check_vma=False,
    )
```

```python
import math

import jax
import jax.numpy as jnp
from jax import lax
from jax.experimental import pallas as pl
from jax.experimental.pallas import tpu as pltpu
from jax.sharding import PartitionSpec as P

HEAD_SIZE = 128
EPSILON = 1e-06
REQS = 32
STEPS = 4
ROWS = 2 * STEPS
LANES = 128
HALF = 1024
QUARTER = 512
RANK = 512
STATE = 16
PAGES = 8
BIG = 60
UNROLL = 8
CHUNKS = 4
PAGE_TOKENS = 16
PROJ = RANK + 2 * STATE
SEND = HALF + QUARTER + HEAD_SIZE
BACK = HALF + QUARTER
F32 = jnp.float32
BF16 = jnp.bfloat16


def vmem():
    return pl.BlockSpec(memory_space=pltpu.VMEM)


def anywhere():
    return pl.BlockSpec(memory_space=pl.ANY)


def smem():
    return pl.BlockSpec(memory_space=pltpu.SMEM)


def params(mib):
    return pltpu.CompilerParams(vmem_limit_bytes=mib * 1024 * 1024)


def cost(mb):
    return pl.CostEstimate(
        flops=3_500_000_000, bytes_accessed=mb * 1_000_000, transcendentals=300_000
    )


def sublanes(shape):
    return lax.broadcasted_iota(jnp.int32, shape, len(shape) - 2)


def pack_kernel(x_hbm, q_hbm, kv_hbm, out_hbm, x_ref, q_ref, kv_ref, rows, out_ref, sems, out_sems):
    groups = range(0, REQS, 16)
    copies = []
    for group in groups:
        span = pl.ds(group, 16)
        trio = ((x_hbm, x_ref), (q_hbm, q_ref), (kv_hbm, kv_ref))
        copies.append(
            [
                pltpu.make_async_copy(
                    far.at[:, span], near.at[:, span], sems.at[index, group // 16]
                )
                for index, (far, near) in enumerate(trio)
            ]
        )
        for copy in copies[-1]:
            copy.start()
    outs = []
    for group in groups:
        for copy in copies[group // 16]:
            copy.wait()
        for step in range(STEPS):
            for half in range(2):
                first = half * STEPS + step
                places = [
                    pl.ds((group + part * 8) * ROWS + first, 8, stride=ROWS) for part in range(2)
                ]
                tile = 0
                for ref, width in ((x_ref, HALF), (q_ref, QUARTER)):
                    block = ref[step, group : group + 16, half * width : (half + 1) * width]
                    block = block.astype(F32)
                    for column in range(0, width, LANES):
                        rows[tile, places[0], :] = block[0:8, column : column + LANES]
                        rows[tile, places[1], :] = block[8:16, column : column + LANES]
                        tile += 1
            for req in range(group, group + 16):
                rows[SEND // LANES - 1, pl.ds(req * ROWS + step, 2, stride=STEPS), :] = kv_ref[
                    step, req
                ].astype(F32)
        for req in range(group, group + 16):
            for tile in range(SEND // LANES):
                out_ref[req, :, tile * LANES : (tile + 1) * LANES] = rows[
                    tile, req * ROWS : (req + 1) * ROWS, :
                ].astype(BF16)
        span = pl.ds(group, 16)
        outs.append(
            pltpu.make_async_copy(out_ref.at[span], out_hbm.at[span], out_sems.at[group // 16])
        )
        outs[-1].start()
    for copy in outs:
        copy.wait()


def pack(mamba_x, queries, new_kv):
    return pl.pallas_call(
        pack_kernel,
        out_shape=jax.ShapeDtypeStruct((REQS, ROWS, SEND), BF16),
        in_specs=[anywhere()] * 3,
        out_specs=anywhere(),
        scratch_shapes=[
            pltpu.VMEM((STEPS, REQS, 2 * HALF), BF16),
            pltpu.VMEM((STEPS, REQS, 2 * QUARTER), BF16),
            pltpu.VMEM((STEPS, REQS, 2, HEAD_SIZE), BF16),
            pltpu.VMEM((SEND // LANES, REQS * ROWS, LANES), F32),
            pltpu.VMEM((REQS, ROWS, SEND), BF16),
            pltpu.SemaphoreType.DMA((3, 2)),
            pltpu.SemaphoreType.DMA((2,)),
        ],
        compiler_params=params(BIG),
        name="pack",
    )(mamba_x, queries, new_kv)


def halves(ref, row, width):
    low = jnp.broadcast_to(ref[row : row + 1, 0:width], (STEPS, width))
    high = jnp.broadcast_to(ref[row : row + 1, width : 2 * width], (STEPS, width))
    return jnp.concatenate([low, high], axis=0)


def conv_kernel(
    order_ref,
    core_ref,
    rows_hbm,
    past_hbm,
    weight_hbm,
    bias_hbm,
    proj_hbm,
    act_hbm,
    mine_ref,
    other_ref,
    rows_ref,
    past_ref,
    weight_ref,
    bias_ref,
    proj_ref,
    taps,
    past_rows,
    act_ref,
    part,
    sems,
    rows_sems,
    act_sem,
):
    small = [
        pltpu.make_async_copy(far, near, sems.at[index])
        for index, (far, near) in enumerate(
            ((past_hbm, past_ref), (weight_hbm, weight_ref), (bias_hbm, bias_ref))
        )
    ]
    chunk = REQS // CHUNKS
    arriving = [
        pltpu.make_async_copy(
            rows_hbm.at[pl.ds(index * chunk, chunk), :, pl.ds(0, HALF)],
            rows_ref.at[pl.ds(index * chunk, chunk)],
            rows_sems.at[index],
        )
        for index in range(CHUNKS)
    ]
    proj_copy = pltpu.make_async_copy(proj_hbm, proj_ref, sems.at[3])
    for copy in small + arriving + [proj_copy]:
        copy.start()
    for copy in small:
        copy.wait()
    step_of = lax.rem(sublanes((ROWS, HALF)), STEPS)
    for tap in range(3):
        for half in range(2):
            for tile in range(HALF // LANES):
                column = half * HALF + tile * LANES
                block = past_ref[tap, :, column : column + LANES].astype(F32)
                for group in range(0, REQS, 8):
                    place = pl.ds(group * ROWS + (1 - half) * STEPS + 1 + tap, 8, stride=ROWS)
                    past_rows[tile, place, :] = block[group : group + 8]
    taps[0] = halves(bias_ref, 0, HALF)
    for back in range(4):
        taps[1 + back] = halves(weight_ref, 3 - back, HALF)

    def one(req):
        now = rows_ref[req].astype(F32)
        first = pl.multiple_of(order_ref[req] * ROWS, ROWS)
        past = jnp.concatenate(
            [past_rows[tile, pl.ds(first, ROWS), :] for tile in range(HALF // LANES)], axis=1
        )
        total = taps[0] + taps[1] * now
        for back in range(1, 4):
            mixed = jnp.where(step_of >= STEPS - back, past, now)
            total = total + taps[1 + back] * pltpu.roll(mixed, back, 0)
        return total * jax.nn.sigmoid(total)

    def pair(index, carry):
        both = jnp.concatenate([one(2 * index), one(2 * index + 1)], axis=0)
        act_ref[pl.ds(pl.multiple_of(index * 16, 16), 16), :] = both.astype(BF16)
        return carry

    for index in range(CHUNKS):
        arriving[index].wait()
        lax.fori_loop(index * chunk // 2, (index + 1) * chunk // 2, pair, 0)
    act_copy = pltpu.make_async_copy(act_ref, act_hbm, act_sem)
    act_copy.start()
    proj_copy.wait()
    act = act_ref[...]
    low = jnp.dot(act, proj_ref[0:HALF, :], preferred_element_type=F32)
    high = jnp.dot(act, proj_ref[HALF : 2 * HALF, :], preferred_element_type=F32)
    upper = sublanes((ROWS, PROJ)) < STEPS
    for index in range(REQS // 2):
        even = slice(index * 16, index * 16 + 8)
        odd = slice(index * 16 + 8, index * 16 + 16)
        own = jnp.where(upper, low[even], high[odd])
        cross = jnp.where(upper, low[odd], high[even])
        part[index * 8 : index * 8 + 8, :] = own + pltpu.roll(cross, STEPS, 0)
    core = core_ref[0]
    size = REQS * STEPS // 2
    mine_ref[...] = part[pl.ds(pl.multiple_of(core * size, size), size), :]
    other_ref[...] = part[pl.ds(pl.multiple_of((1 - core) * size, size), size), :]
    act_copy.wait()


def convolve(order, core, arrived, conv_state, conv_weight, conv_bias, x_proj):
    half_rows = jax.ShapeDtypeStruct((REQS * STEPS // 2, PROJ), F32)
    return pl.pallas_call(
        conv_kernel,
        out_shape=(jax.ShapeDtypeStruct((REQS * ROWS, HALF), BF16), half_rows, half_rows),
        in_specs=[smem(), smem()] + [anywhere()] * 5,
        out_specs=(anywhere(), vmem(), vmem()),
        scratch_shapes=[
            pltpu.VMEM((REQS, ROWS, HALF), BF16),
            pltpu.VMEM(conv_state.shape, BF16),
            pltpu.VMEM(conv_weight.shape, F32),
            pltpu.VMEM(conv_bias.shape, F32),
            pltpu.VMEM(x_proj.shape, BF16),
            pltpu.VMEM((5, ROWS, HALF), F32),
            pltpu.VMEM((HALF // LANES, REQS * ROWS, LANES), F32),
            pltpu.VMEM((REQS * ROWS, HALF), BF16),
            pltpu.VMEM((REQS * STEPS, PROJ), F32),
            pltpu.SemaphoreType.DMA((4,)),
            pltpu.SemaphoreType.DMA((CHUNKS,)),
            pltpu.SemaphoreType.DMA,
        ],
        compiler_params=params(56),
        name="convolve",
    )(order, core, arrived, conv_state, conv_weight, conv_bias, x_proj)


def norm_kernel(sum_ref, one_ref, two_ref, three_ref, gain_ref, after_ref, out_ref):
    del after_ref
    total = (
        sum_ref[...]
        + one_ref[...].astype(F32)
        + two_ref[...].astype(F32)
        + three_ref[...].astype(F32)
    )
    low = total[:, :RANK]
    spread = lax.rsqrt(jnp.mean(low * low, axis=-1, keepdims=True) + EPSILON)
    out_ref[:, 0:RANK] = (low * spread * gain_ref[...]).astype(BF16)
    coef = total[:, RANK:]
    coef = jnp.concatenate([coef, jnp.zeros((coef.shape[0], LANES - 2 * STATE), F32)], axis=1)
    coef_high = coef.astype(BF16)
    out_ref[:, RANK : RANK + LANES] = coef_high
    out_ref[:, RANK + LANES :] = (coef - coef_high.astype(F32)).astype(BF16)


def normalise(chip_sum, ring, gain, after):
    return pl.pallas_call(
        norm_kernel,
        out_shape=jax.ShapeDtypeStruct((REQS * STEPS // 2, RANK + 2 * LANES), BF16),
        in_specs=[vmem()] * 5 + [anywhere()],
        out_specs=vmem(),
        compiler_params=params(8),
        name="normalise",
    )(chip_sum, *ring, gain, after)


def attend_kernel(
    order_ref, table_ref, length_ref, rows_ref, pool_ref, out_ref, scores_ref, weights_ref, inverse_ref
):
    scale = 1.0 / math.sqrt(HEAD_SIZE)
    count = 4 * ROWS
    wide = (count, 2 * LANES)
    lane = lax.broadcasted_iota(jnp.int32, wide, 1)
    step_of = lax.rem(lax.broadcasted_iota(jnp.int32, wide, 0), STEPS)
    fresh_ok = (lane >= LANES) & (lane - LANES <= step_of)
    pad = jnp.zeros((LANES - PAGE_TOKENS, HEAD_SIZE), BF16)
    blank = jnp.zeros((ROWS, HEAD_SIZE), F32)

    def score(req):
        source = order_ref[req]
        query = rows_ref[req, :, HALF : HALF + QUARTER].astype(F32)
        query = jnp.concatenate(
            [query[:, h * HEAD_SIZE : (h + 1) * HEAD_SIZE] for h in range(4)], axis=0
        ).astype(BF16)
        fresh = rows_ref[req, :, HALF + QUARTER : SEND].astype(F32)
        fresh = jnp.concatenate([fresh, blank], axis=0).astype(BF16)
        keys = [pool_ref[table_ref[source, page], 0] for page in range(PAGES)]
        keys = jnp.concatenate(keys + [fresh, pad], axis=0)
        scores_ref[req] = (
            lax.dot_general(query, keys, (((1,), (1,)), ((), ())), preferred_element_type=F32)
            * scale
        )

    def soften(req):
        length = length_ref[order_ref[req]]
        valid = (lane < length) & (lane < LANES) | fresh_ok
        scores = jnp.where(valid, scores_ref[req], -jnp.inf)
        weights = jnp.exp(scores - jnp.max(scores, axis=1, keepdims=True))
        total = jnp.sum(weights, axis=1, keepdims=True)
        weights_ref[req] = weights.astype(BF16)
        inverse_ref[req] = jnp.broadcast_to(1.0 / total, (count, LANES))

    def mix(req):
        source = order_ref[req]
        fresh = rows_ref[req, :, HALF + QUARTER : SEND].astype(F32)
        fresh = jnp.concatenate([pltpu.roll(fresh, STEPS, 0), blank], axis=0).astype(BF16)
        values = [pool_ref[table_ref[source, page], 1] for page in range(PAGES)]
        values = jnp.concatenate(values + [fresh, pad], axis=0)
        mixed = jnp.dot(weights_ref[req], values, preferred_element_type=F32) * inverse_ref[req]
        for h in range(4):
            out_ref[req, :, h * HEAD_SIZE : (h + 1) * HEAD_SIZE] = mixed[
                h * ROWS : (h + 1) * ROWS
            ].astype(BF16)

    for phase in (score, soften, mix):

        def some(index, carry, phase=phase):
            for offset in range(UNROLL):
                phase(UNROLL * index + offset)
            return carry

        lax.fori_loop(0, REQS // UNROLL, some, 0)


def attend(order, page_table, prompt_len, arrived, pool):
    return pl.pallas_call(
        attend_kernel,
        out_shape=jax.ShapeDtypeStruct((REQS, ROWS, QUARTER), BF16),
        in_specs=[smem()] * 3 + [vmem()] * 2,
        out_specs=vmem(),
        scratch_shapes=[
            pltpu.VMEM((REQS, 4 * ROWS, 2 * LANES), F32),
            pltpu.VMEM((REQS, 4 * ROWS, 2 * LANES), BF16),
            pltpu.VMEM((REQS, 4 * ROWS, LANES), F32),
        ],
        compiler_params=params(8),
        cost_estimate=cost(6),
        name="attend",
    )(order, page_table, prompt_len, arrived, pool)


def gather_rows(parts, sub):
    four = sub < 4
    parts = [
        jnp.where(four, parts[s], parts[s + 4])
        + pltpu.roll(jnp.where(four, parts[s + 4], parts[s]), 4, 0)
        for s in range(4)
    ]
    two = lax.rem(sub, 4) < 2
    parts = [
        jnp.where(
            two,
            parts[s] + pltpu.roll(parts[s], 6, 0),
            parts[s + 2] + pltpu.roll(parts[s + 2], 2, 0),
        )
        for s in range(2)
    ]
    return jnp.where(
        lax.rem(sub, 2) < 1,
        parts[0] + pltpu.roll(parts[0], 7, 0),
        parts[1] + pltpu.roll(parts[1], 1, 0),
    )


def scan_kernel(
    order_ref,
    core_ref,
    ours_ref,
    theirs_ref,
    act_ref,
    attended_ref,
    state_ref,
    dt_proj_ref,
    dt_bias_ref,
    a_log_ref,
    skip_ref,
    out_ref,
    packed,
    rate,
    fed,
    decay,
    skip,
    coef,
):
    core = core_ref[0]
    size = REQS * STEPS // 2
    packed[pl.ds(pl.multiple_of(core * size, size), size), :] = ours_ref[...]
    packed[pl.ds(pl.multiple_of((1 - core) * size, size), size), :] = theirs_ref[...]
    skip[...] = halves(skip_ref, 0, HALF)
    decay[...] = jnp.exp(a_log_ref[...]) * (-1.0 / math.log(2.0))
    coef[...] = jnp.transpose(
        packed[:, RANK : RANK + LANES].astype(F32) + packed[:, RANK + LANES :].astype(F32)
    )
    upper = sublanes((ROWS, HALF)) < STEPS
    normed = packed[:, 0:RANK]
    low = jnp.dot(normed, dt_proj_ref[:, 0:HALF], preferred_element_type=F32)
    low = jax.nn.softplus(low + dt_bias_ref[:, 0:HALF])
    high = jnp.dot(normed, dt_proj_ref[:, HALF:], preferred_element_type=F32)
    high = jax.nn.softplus(high + dt_bias_ref[:, HALF:])
    for index in range(REQS // 2):
        rows = slice(index * 8, index * 8 + 8)
        even = jnp.where(upper, low[rows], pltpu.roll(high[rows], STEPS, 0))
        odd = jnp.where(upper, pltpu.roll(low[rows], STEPS, 0), high[rows])
        both = jnp.concatenate([even, odd], axis=0)
        span = slice(index * 16, index * 16 + 16)
        both_fed = both * act_ref[span, :].astype(F32)
        rate[2 * index] = even
        rate[2 * index + 1] = odd
        fed[2 * index] = both_fed[0:8]
        fed[2 * index + 1] = both_fed[8:16]
    sub = sublanes((ROWS, LANES))

    def one(req, act):
        source = order_ref[req]
        turned = pltpu.roll(coef[0 : 2 * STATE, :], lax.rem(LANES - STEPS * req, LANES), 1)
        into = [
            jnp.broadcast_to(turned[0:STATE, s : s + 1], (STATE, LANES)) for s in range(STEPS)
        ]
        read = [
            jnp.broadcast_to(turned[STATE : 2 * STATE, s : s + 1], (STATE, LANES))
            for s in range(STEPS)
        ]
        for tile in range(HALF // LANES):
            place = slice(tile * LANES, (tile + 1) * LANES)
            parts = []
            for half in range(2):
                columns = slice(half * HALF + tile * LANES, half * HALF + (tile + 1) * LANES)
                hidden = state_ref[source, :, columns]
                slope = decay[:, columns]
                for step in range(STEPS):
                    row = slice(half * STEPS + step, half * STEPS + step + 1)
                    hidden = (
                        jnp.exp2(jnp.broadcast_to(rate[req, row, place], (STATE, LANES)) * slope) * hidden
                        + jnp.broadcast_to(fed[req, row, place], (STATE, LANES)) * into[step]
                    )
                    seen = hidden * read[step]
                    parts.append(seen[0:8] + seen[8:16])
            summed = gather_rows(parts, sub) + skip[:, place] * act[:, place]
            out_ref[req, :, place] = summed.astype(BF16)
        out_ref[req, :, HALF:BACK] = attended_ref[req]

    def pair(index, carry):
        act = act_ref[pl.ds(pl.multiple_of(index * 16, 16), 16), :].astype(F32)
        one(2 * index, act[0:8])
        one(2 * index + 1, act[8:16])
        return carry

    lax.fori_loop(0, REQS // 2, pair, 0)


def scan(order, core, ours, theirs, act, attended, ssm_state, dt_proj, dt_bias, a_log, skip_d):
    return pl.pallas_call(
        scan_kernel,
        out_shape=jax.ShapeDtypeStruct((REQS, ROWS, BACK), BF16),
        in_specs=[smem(), smem()] + [vmem()] * 9,
        out_specs=vmem(),
        scratch_shapes=[
            pltpu.VMEM((REQS * STEPS, RANK + 2 * LANES), BF16),
            pltpu.VMEM((REQS, ROWS, HALF), F32),
            pltpu.VMEM((REQS, ROWS, HALF), F32),
            pltpu.VMEM((STATE, 2 * HALF), F32),
            pltpu.VMEM((ROWS, HALF), F32),
            pltpu.VMEM((LANES, LANES), F32),
        ],
        compiler_params=params(16),
        name="scan",
    )(order, core, ours, theirs, act, attended, ssm_state, dt_proj, dt_bias, a_log, skip_d)


def unpack_kernel(back_ref, z_ref, attn_ref, mamba_ref, rows):
    for req in range(REQS):
        for tile in range(BACK // LANES):
            rows[tile, req * ROWS : (req + 1) * ROWS, :] = back_ref[
                req, :, tile * LANES : (tile + 1) * LANES
            ].astype(F32)
    for step in range(STEPS):
        for group in range(0, REQS, 16):
            for half in range(2):
                first = half * STEPS + step
                places = [
                    pl.ds((group + part * 8) * ROWS + first, 8, stride=ROWS) for part in range(2)
                ]
                for tile in range(BACK // LANES):
                    block = jnp.concatenate([rows[tile, place, :] for place in places], axis=0)
                    if tile < HALF // LANES:
                        first_column = half * HALF + tile * LANES
                        columns = slice(first_column, first_column + LANES)
                        z = z_ref[step, group : group + 16, columns].astype(F32)
                        block = block * (z * jax.nn.sigmoid(z))
                        mamba_ref[step, group : group + 16, columns] = block.astype(BF16)
                    else:
                        first_column = half * QUARTER + tile * LANES - HALF
                        columns = slice(first_column, first_column + LANES)
                        attn_ref[step, group : group + 16, columns] = block.astype(BF16)


def unpack(back, mamba_z):
    return pl.pallas_call(
        unpack_kernel,
        out_shape=(
            jax.ShapeDtypeStruct((STEPS, REQS, 2 * QUARTER), BF16),
            jax.ShapeDtypeStruct((STEPS, REQS, 2 * HALF), BF16),
        ),
        in_specs=[vmem()] * 2,
        out_specs=(vmem(), vmem()),
        scratch_shapes=[pltpu.VMEM((BACK // LANES, REQS * ROWS, LANES), F32)],
        compiler_params=params(24),
        name="unpack",
    )(back, mamba_z)


def per_device(
    queries,
    new_kv,
    prefill_page_pool,
    page_table,
    prompt_len,
    dest_device,
    ssm_state,
    conv_state,
    mamba_x,
    mamba_z,
    conv_weight,
    conv_bias,
    x_proj,
    dt_gain,
    dt_proj,
    dt_bias,
    a_log,
    skip_d,
):
    slots = jnp.arange(REQS, dtype=jnp.int32)
    order = jnp.sum(
        jnp.where(dest_device[None, :] == slots[:, None], slots[None, :], 0), axis=1
    )
    core = (lax.axis_index("tp") % 2).astype(jnp.int32).reshape(1)
    swap = [(j, j ^ 1) for j in range(8)]

    outgoing = pack(mamba_x, queries, new_kv)
    arrived = lax.all_to_all(outgoing, "req", split_axis=0, concat_axis=0, tiled=True)
    act, mine, other = convolve(
        order,
        core,
        arrived,
        jnp.transpose(conv_state, (1, 0, 2)),
        conv_weight,
        conv_bias[None],
        x_proj,
    )
    unit = jnp.where(order[0] >= 0, 1, 2).astype(BF16)
    pool = prefill_page_pool * unit
    chip_sum = mine + lax.ppermute(other, "tp", swap)
    small = chip_sum.astype(BF16)
    ring = [
        lax.ppermute(small, "tp", [(j, (j + hop) % 8) for j in range(8)]) for hop in (2, 6, 4)
    ]
    attended = attend(order, page_table, prompt_len, arrived, pool)
    ours = normalise(chip_sum, ring, dt_gain[None], attended)
    theirs = lax.ppermute(ours, "tp", swap)
    returning = scan(
        order,
        core,
        ours,
        theirs,
        act,
        attended,
        ssm_state,
        dt_proj,
        dt_bias[None],
        a_log,
        skip_d[None],
    )
    back = lax.all_to_all(returning, "req", split_axis=0, concat_axis=0, tiled=True)
    return unpack(back, mamba_z)


def solution(mesh):
    return jax.shard_map(
        per_device,
        mesh=mesh,
        in_specs=(
            P(None, "req", "tp"),
            P(None, "req", None, "tp"),
            P("req", None, None, "tp"),
            P("req", None),
            P("req"),
            P("req"),
            P("req", None, "tp"),
            P("req", None, "tp"),
            P(None, "req", "tp"),
            P(None, "req", "tp"),
            P(None, "tp"),
            P("tp"),
            P("tp", None),
            P(),
            P(None, "tp"),
            P("tp"),
            P(None, "tp"),
            P("tp"),
        ),
        out_specs=(P(None, "req", "tp"), P(None, "req", "tp")),
        check_vma=False,
    )
```

```python
import math

import jax
import jax.numpy as jnp
from jax import lax
from jax.experimental import pallas as pl
from jax.experimental.pallas import tpu as pltpu
from jax.sharding import PartitionSpec as P

HEAD_SIZE = 128
EPSILON = 1e-06
REQS = 32
STEPS = 4
ROWS = 2 * STEPS
LANES = 128
HALF = 1024
QUARTER = 512
RANK = 512
STATE = 16
PAGES = 8
WHOLE = 63
BIG = 60
UNROLL = 32
KEEPS = 4
CHUNKS = 4
PAGE_TOKENS = 16
PROJ = RANK + 2 * STATE
SEND = HALF + QUARTER + HEAD_SIZE
BACK = HALF + QUARTER
F32 = jnp.float32
BF16 = jnp.bfloat16


def vmem():
    return pl.BlockSpec(memory_space=pltpu.VMEM)


def anywhere():
    return pl.BlockSpec(memory_space=pl.ANY)


def smem():
    return pl.BlockSpec(memory_space=pltpu.SMEM)


def params(mib):
    return pltpu.CompilerParams(vmem_limit_bytes=mib * 1024 * 1024)


def cost(mb):
    return pl.CostEstimate(
        flops=3_500_000_000, bytes_accessed=mb * 1_000_000, transcendentals=300_000
    )


def softplus(x):
    return jnp.maximum(x, 0.0) + jnp.log(1.0 + jnp.exp(-jnp.abs(x)))


def silu(x):
    half = 0.5 * x
    return half * jnp.tanh(half) + half


def sublanes(shape):
    return lax.broadcasted_iota(jnp.int32, shape, len(shape) - 2)


def pack_kernel(x_hbm, q_hbm, kv_hbm, out_hbm, x_ref, q_ref, kv_ref, rows, out_ref, sems, out_sems):
    groups = range(0, REQS, 16)
    copies = []
    for group in groups:
        span = pl.ds(group, 16)
        trio = ((x_hbm, x_ref), (q_hbm, q_ref), (kv_hbm, kv_ref))
        copies.append(
            [
                pltpu.make_async_copy(
                    far.at[:, span], near.at[:, span], sems.at[index, group // 16]
                )
                for index, (far, near) in enumerate(trio)
            ]
        )
        for copy in copies[-1]:
            copy.start()
    outs = []
    for group in groups:
        for copy in copies[group // 16]:
            copy.wait()
        for step in range(STEPS):
            for half in range(2):
                first = half * STEPS + step
                places = [
                    pl.ds((group + part * 8) * ROWS + first, 8, stride=ROWS) for part in range(2)
                ]
                tile = 0
                for ref, width in ((x_ref, HALF), (q_ref, QUARTER)):
                    block = ref[step, group : group + 16, half * width : (half + 1) * width]
                    block = block.astype(F32)
                    for column in range(0, width, LANES):
                        rows[tile, places[0], :] = block[0:8, column : column + LANES]
                        rows[tile, places[1], :] = block[8:16, column : column + LANES]
                        tile += 1
            for req in range(group, group + 16):
                rows[SEND // LANES - 1, pl.ds(req * ROWS + step, 2, stride=STEPS), :] = kv_ref[
                    step, req
                ].astype(F32)
        for req in range(group, group + 16):
            for tile in range(SEND // LANES):
                out_ref[req, :, tile * LANES : (tile + 1) * LANES] = rows[
                    tile, req * ROWS : (req + 1) * ROWS, :
                ].astype(BF16)
        span = pl.ds(group, 16)
        outs.append(
            pltpu.make_async_copy(out_ref.at[span], out_hbm.at[span], out_sems.at[group // 16])
        )
        outs[-1].start()
    for copy in outs:
        copy.wait()


def pack(mamba_x, queries, new_kv):
    return pl.pallas_call(
        pack_kernel,
        out_shape=jax.ShapeDtypeStruct((REQS, ROWS, SEND), BF16),
        in_specs=[anywhere()] * 3,
        out_specs=anywhere(),
        scratch_shapes=[
            pltpu.VMEM((STEPS, REQS, 2 * HALF), BF16),
            pltpu.VMEM((STEPS, REQS, 2 * QUARTER), BF16),
            pltpu.VMEM((STEPS, REQS, 2, HEAD_SIZE), BF16),
            pltpu.VMEM((SEND // LANES, REQS * ROWS, LANES), F32),
            pltpu.VMEM((REQS, ROWS, SEND), BF16),
            pltpu.SemaphoreType.DMA((3, 2)),
            pltpu.SemaphoreType.DMA((2,)),
        ],
        compiler_params=params(BIG),
        name="pack",
    )(mamba_x, queries, new_kv)


def halves(ref, row, width):
    low = jnp.broadcast_to(ref[row : row + 1, 0:width], (STEPS, width))
    high = jnp.broadcast_to(ref[row : row + 1, width : 2 * width], (STEPS, width))
    return jnp.concatenate([low, high], axis=0)


def stage_kernel(order_ref, sent_ref, past_ref, weight_ref, bias_ref, out_ref, past_rows, past_taps):
    del sent_ref
    step_of = lax.rem(sublanes((ROWS, HALF)), STEPS)
    for tap in range(3):
        for half in range(2):
            for tile in range(HALF // LANES):
                column = half * HALF + tile * LANES
                block = past_ref[tap, :, column : column + LANES].astype(F32)
                for group in range(0, REQS, 8):
                    place = pl.ds(group * ROWS + (1 - half) * STEPS + 1 + tap, 8, stride=ROWS)
                    past_rows[tile, place, :] = block[group : group + 8]
    plain = [halves(weight_ref, tap, HALF) for tap in range(4)]
    for back in range(4):
        out_ref[REQS + back] = jnp.where(step_of >= back, plain[3 - back], 0.0)
        past_taps[back] = plain[3 - back]
    past_taps[0] = halves(bias_ref, 0, HALF)

    def one(req, carry):
        first = pl.multiple_of(order_ref[req] * ROWS, ROWS)
        past = jnp.concatenate(
            [past_rows[tile, pl.ds(first, ROWS), :] for tile in range(HALF // LANES)], axis=1
        )
        total = past_taps[0]
        for back in range(1, 4):
            moved = jnp.where(step_of < back, pltpu.roll(past, back, 0), 0.0)
            total = total + past_taps[back] * moved
        out_ref[req] = total
        return carry

    lax.fori_loop(0, REQS, one, 0)


def stage(order, sent, conv_state, conv_weight, conv_bias):
    return pl.pallas_call(
        stage_kernel,
        out_shape=jax.ShapeDtypeStruct((REQS + 4, ROWS, HALF), F32),
        in_specs=[smem(), anywhere()] + [vmem()] * 3,
        out_specs=vmem(),
        scratch_shapes=[
            pltpu.VMEM((HALF // LANES, REQS * ROWS, LANES), F32),
            pltpu.VMEM((4, ROWS, HALF), F32),
        ],
        compiler_params=pltpu.CompilerParams(vmem_limit_bytes=(64 * 1024 - 600) * 1024),
        name="stage",
    )(order, sent, conv_state, conv_weight, conv_bias)


def conv_kernel(
    core_ref,
    rows_hbm,
    prior_hbm,
    proj_hbm,
    act_hbm,
    mine_ref,
    other_ref,
    rows_ref,
    prior_ref,
    proj_ref,
    act_ref,
    part,
    rows_sems,
    prior_sems,
    proj_sem,
    act_sem,
):
    chunk = REQS // CHUNKS
    arriving = [
        pltpu.make_async_copy(
            prior_hbm.at[pl.ds(REQS, 4)], prior_ref.at[pl.ds(REQS, 4)], prior_sems.at[CHUNKS]
        )
    ]
    for index in range(CHUNKS):
        span = pl.ds(index * chunk, chunk)
        arriving.append(
            pltpu.make_async_copy(
                rows_hbm.at[span, :, pl.ds(0, HALF)], rows_ref.at[span], rows_sems.at[index]
            )
        )
        arriving.append(
            pltpu.make_async_copy(prior_hbm.at[span], prior_ref.at[span], prior_sems.at[index])
        )
    proj_copy = pltpu.make_async_copy(proj_hbm, proj_ref, proj_sem)
    for copy in arriving + [proj_copy]:
        copy.start()
    arriving[0].wait()

    def one(req):
        now = rows_ref[req].astype(F32)
        total = prior_ref[req] + prior_ref[REQS] * now
        for back in range(1, 4):
            total = total + prior_ref[REQS + back] * pltpu.roll(now, back, 0)
        return silu(total)

    def pair(index, carry):
        both = jnp.concatenate([one(2 * index), one(2 * index + 1)], axis=0)
        act_ref[pl.ds(pl.multiple_of(index * 16, 16), 16), :] = both.astype(BF16)
        return carry

    for index in range(CHUNKS):
        arriving[1 + 2 * index].wait()
        arriving[2 + 2 * index].wait()
        lax.fori_loop(index * chunk // 2, (index + 1) * chunk // 2, pair, 0)
    act_copy = pltpu.make_async_copy(act_ref, act_hbm, act_sem)
    act_copy.start()
    proj_copy.wait()
    act = act_ref[...]
    low = jnp.dot(act, proj_ref[0:HALF, :], preferred_element_type=F32)
    high = jnp.dot(act, proj_ref[HALF : 2 * HALF, :], preferred_element_type=F32)
    upper = sublanes((ROWS, PROJ)) < STEPS
    for index in range(REQS // 2):
        even = slice(index * 16, index * 16 + 8)
        odd = slice(index * 16 + 8, index * 16 + 16)
        own = jnp.where(upper, low[even], high[odd])
        cross = jnp.where(upper, low[odd], high[even])
        part[index * 8 : index * 8 + 8, :] = own + pltpu.roll(cross, STEPS, 0)
    core = core_ref[0]
    size = REQS * STEPS // 2
    mine_ref[...] = part[pl.ds(pl.multiple_of(core * size, size), size), :]
    other_ref[...] = part[pl.ds(pl.multiple_of((1 - core) * size, size), size), :]
    act_copy.wait()


def convolve(core, arrived, prior, x_proj):
    half_rows = jax.ShapeDtypeStruct((REQS * STEPS // 2, PROJ), F32)
    return pl.pallas_call(
        conv_kernel,
        out_shape=(jax.ShapeDtypeStruct((REQS * ROWS, HALF), BF16), half_rows, half_rows),
        in_specs=[smem()] + [anywhere()] * 3,
        out_specs=(anywhere(), vmem(), vmem()),
        scratch_shapes=[
            pltpu.VMEM((REQS, ROWS, HALF), BF16),
            pltpu.VMEM(prior.shape, F32),
            pltpu.VMEM(x_proj.shape, BF16),
            pltpu.VMEM((REQS * ROWS, HALF), BF16),
            pltpu.VMEM((REQS * STEPS, PROJ), F32),
            pltpu.SemaphoreType.DMA((CHUNKS,)),
            pltpu.SemaphoreType.DMA((CHUNKS + 1,)),
            pltpu.SemaphoreType.DMA,
            pltpu.SemaphoreType.DMA,
        ],
        compiler_params=params(BIG),
        name="convolve",
    )(core, arrived, prior, x_proj)


def norm_kernel(sum_ref, one_ref, two_ref, three_ref, gain_ref, after_ref, out_ref):
    del after_ref
    total = (
        sum_ref[...]
        + one_ref[...].astype(F32)
        + two_ref[...].astype(F32)
        + three_ref[...].astype(F32)
    )
    low = total[:, :RANK]
    spread = lax.rsqrt(jnp.mean(low * low, axis=-1, keepdims=True) + EPSILON)
    out_ref[:, 0:RANK] = (low * spread * gain_ref[...]).astype(BF16)
    coef = total[:, RANK:]
    coef = jnp.concatenate([coef, jnp.zeros((coef.shape[0], LANES - 2 * STATE), F32)], axis=1)
    coef_high = coef.astype(BF16)
    out_ref[:, RANK : RANK + LANES] = coef_high
    out_ref[:, RANK + LANES :] = (coef - coef_high.astype(F32)).astype(BF16)


def normalise(chip_sum, ring, gain, after):
    return pl.pallas_call(
        norm_kernel,
        out_shape=jax.ShapeDtypeStruct((REQS * STEPS // 2, RANK + 2 * LANES), BF16),
        in_specs=[vmem()] * 5 + [anywhere()],
        out_specs=vmem(),
        compiler_params=params(8),
        name="normalise",
    )(chip_sum, *ring, gain, after)


def attend_kernel(
    order_ref, table_ref, length_ref, rows_ref, pool_ref, out_ref, scores_ref, weights_ref
):
    scale = math.log2(math.e) / math.sqrt(HEAD_SIZE)
    count = 4 * ROWS
    lane = lax.broadcasted_iota(jnp.int32, (count, LANES), 1)
    step_of = lax.rem(lax.broadcasted_iota(jnp.int32, (count, LANES), 0), STEPS)
    fresh_ok = lane <= step_of
    pad = jnp.zeros((LANES - PAGE_TOKENS, HEAD_SIZE), BF16)
    blank = jnp.zeros((ROWS, HEAD_SIZE), F32)
    ones = jnp.ones((2 * LANES, LANES), BF16)

    def score(req):
        source = order_ref[req]
        query = rows_ref[req, :, HALF : HALF + QUARTER].astype(F32)
        query = jnp.concatenate(
            [query[:, h * HEAD_SIZE : (h + 1) * HEAD_SIZE] for h in range(4)], axis=0
        ).astype(BF16)
        fresh = rows_ref[req, :, HALF + QUARTER : SEND].astype(F32)
        fresh = jnp.concatenate([fresh, blank], axis=0).astype(BF16)
        keys = [pool_ref[table_ref[source, page], 0] for page in range(PAGES)]
        keys = jnp.concatenate(keys + [fresh, pad], axis=0)
        scores_ref[req] = lax.dot_general(
            query, keys, (((1,), (1,)), ((), ())), preferred_element_type=F32
        )

    def soften(req):
        length = length_ref[order_ref[req]]
        old = jnp.where(lane < length, scores_ref[req, :, 0:LANES] * scale, -jnp.inf)
        new = jnp.where(fresh_ok, scores_ref[req, :, LANES:] * scale, -jnp.inf)
        top = jnp.max(jnp.maximum(old, new), axis=1, keepdims=True)
        weights_ref[req, :, 0:LANES] = jnp.exp2(old - top).astype(BF16)
        weights_ref[req, :, LANES:] = jnp.exp2(new - top).astype(BF16)

    def mix(req):
        source = order_ref[req]
        fresh = rows_ref[req, :, HALF + QUARTER : SEND].astype(F32)
        fresh = jnp.concatenate([pltpu.roll(fresh, STEPS, 0), blank], axis=0).astype(BF16)
        values = [pool_ref[table_ref[source, page], 1] for page in range(PAGES)]
        values = jnp.concatenate(values + [fresh, pad], axis=0)
        values = jnp.concatenate([values, ones], axis=1)
        mixed = jnp.dot(weights_ref[req], values, preferred_element_type=F32)
        mixed = mixed[:, 0:LANES] / mixed[:, LANES:]
        for h in range(4):
            out_ref[req, :, h * HEAD_SIZE : (h + 1) * HEAD_SIZE] = mixed[
                h * ROWS : (h + 1) * ROWS
            ].astype(BF16)

    for phase in (score, soften, mix):

        def some(index, carry, phase=phase):
            for offset in range(UNROLL):
                phase(UNROLL * index + offset)
            return carry

        lax.fori_loop(0, REQS // UNROLL, some, 0)


def attend(order, page_table, prompt_len, arrived, pool):
    return pl.pallas_call(
        attend_kernel,
        out_shape=jax.ShapeDtypeStruct((REQS, ROWS, QUARTER), BF16),
        in_specs=[smem()] * 3 + [vmem()] * 2,
        out_specs=vmem(),
        scratch_shapes=[
            pltpu.VMEM((REQS, 4 * ROWS, 2 * LANES), F32),
            pltpu.VMEM((REQS, 4 * ROWS, 2 * LANES), BF16),
        ],
        compiler_params=params(8),
        cost_estimate=cost(6),
        name="attend",
    )(order, page_table, prompt_len, arrived, pool)


def scan_kernel(
    order_ref,
    core_ref,
    ours_ref,
    theirs_ref,
    act_ref,
    attended_ref,
    state_ref,
    dt_proj_ref,
    dt_bias_ref,
    a_log_ref,
    skip_ref,
    out_ref,
    packed,
    rate,
    fed,
    decay,
    skip,
    coef,
    read,
    *keeps,
):
    core = core_ref[0]
    size = REQS * STEPS // 2
    packed[pl.ds(pl.multiple_of(core * size, size), size), :] = ours_ref[...]
    packed[pl.ds(pl.multiple_of((1 - core) * size, size), size), :] = theirs_ref[...]
    skip[...] = halves(skip_ref, 0, HALF)
    decay[...] = jnp.exp(a_log_ref[...]) * (-1.0 / math.log(2.0))
    coef[...] = jnp.transpose(
        packed[:, RANK : RANK + LANES].astype(F32) + packed[:, RANK + LANES :].astype(F32)
    )
    upper = sublanes((ROWS, HALF)) < STEPS
    normed = packed[:, 0:RANK]
    low = jnp.dot(normed, dt_proj_ref[:, 0:HALF], preferred_element_type=F32)
    low = softplus(low + dt_bias_ref[:, 0:HALF])
    high = jnp.dot(normed, dt_proj_ref[:, HALF:], preferred_element_type=F32)
    high = softplus(high + dt_bias_ref[:, HALF:])
    for index in range(REQS // 2):
        rows = slice(index * 8, index * 8 + 8)
        even = jnp.where(upper, low[rows], pltpu.roll(high[rows], STEPS, 0))
        odd = jnp.where(upper, pltpu.roll(low[rows], STEPS, 0), high[rows])
        both = jnp.concatenate([even, odd], axis=0)
        span = slice(index * 16, index * 16 + 16)
        both_fed = both * act_ref[span, :].astype(F32)
        rate[2 * index] = even
        rate[2 * index + 1] = odd
        fed[2 * index] = both_fed[0:8]
        fed[2 * index + 1] = both_fed[8:16]
    lane = lax.broadcasted_iota(jnp.int32, (REQS * STEPS, LANES), 1)
    row = lax.broadcasted_iota(jnp.int32, (REQS * STEPS, LANES), 0)
    parts = []
    for first in (RANK, RANK + LANES):
        part = packed[:, first : first + LANES].astype(F32)
        spread = jnp.zeros_like(part)
        for block in range(LANES // STATE):
            moved = pltpu.roll(part, (block * STATE - STATE) % LANES, 1)
            spread = jnp.where(
                (lane // STATE == block) & (lax.rem(row, 2 * STEPS) == block), moved, spread
            )
        parts.append(spread)
    for pair in range(REQS // 2):
        rows = slice(pair * 8, pair * 8 + 8)
        read[pair] = jnp.concatenate([parts[0][rows], parts[1][rows]], axis=0).astype(BF16)
    upper = sublanes((ROWS, LANES)) < STEPS

    def advance(pair, keep):
        for which in range(2):
            req = 2 * pair + which
            source = order_ref[req]
            turned = pltpu.roll(coef[0:STATE, :], lax.rem(LANES - STEPS * req, LANES), 1)
            into = [
                jnp.broadcast_to(turned[:, s : s + 1], (STATE, LANES)) for s in range(STEPS)
            ]
            for first_tile in range(0, HALF // LANES, 2):
                chains = [
                    (tile, half) for tile in range(first_tile, first_tile + 2) for half in range(2)
                ]
                spans = [
                    slice(half * HALF + tile * LANES, half * HALF + (tile + 1) * LANES)
                    for tile, half in chains
                ]
                hidden = [state_ref[source, :, columns] for columns in spans]
                for step in range(STEPS):
                    first = (which * STEPS + step) * STATE
                    for index, (tile, half) in enumerate(chains):
                        place = slice(tile * LANES, (tile + 1) * LANES)
                        line = slice(half * STEPS + step, half * STEPS + step + 1)
                        speed = jnp.broadcast_to(rate[req, line, place], (STATE, LANES))
                        feed = jnp.broadcast_to(fed[req, line, place], (STATE, LANES))
                        hidden[index] = (
                            jnp.exp2(speed * decay[:, spans[index]]) * hidden[index]
                            + feed * into[step]
                        )
                        keep[first : first + STATE, spans[index]] = hidden[index].astype(BF16)

    def readout(pair, keep):
        both = jnp.dot(read[pair], keep[...], preferred_element_type=F32)
        both = both[0:8] + both[8:16]
        act = act_ref[pl.ds(pl.multiple_of(pair * 16, 16), 16), :].astype(F32)
        for tile in range(HALF // LANES):
            place = slice(tile * LANES, (tile + 1) * LANES)
            low = both[:, place]
            high = both[:, HALF + tile * LANES : HALF + (tile + 1) * LANES]
            even = jnp.where(upper, low, pltpu.roll(high, STEPS, 0))
            odd = jnp.where(upper, pltpu.roll(low, STEPS, 0), high)
            out_ref[2 * pair, :, place] = (even + skip[:, place] * act[0:8, place]).astype(BF16)
            out_ref[2 * pair + 1, :, place] = (odd + skip[:, place] * act[8:16, place]).astype(BF16)

    def some(index, carry):
        for offset in range(len(keeps)):
            advance(len(keeps) * index + offset, keeps[offset])
            if offset:
                readout(len(keeps) * index + offset - 1, keeps[offset - 1])
        readout(len(keeps) * index + len(keeps) - 1, keeps[-1])
        return carry

    lax.fori_loop(0, REQS // 2 // len(keeps), some, 0)
    for req in range(REQS):
        out_ref[req, :, HALF:BACK] = attended_ref[req]


def scan(order, core, ours, theirs, act, attended, ssm_state, dt_proj, dt_bias, a_log, skip_d):
    return pl.pallas_call(
        scan_kernel,
        out_shape=jax.ShapeDtypeStruct((REQS, ROWS, BACK), BF16),
        in_specs=[smem(), smem()] + [vmem()] * 9,
        out_specs=vmem(),
        scratch_shapes=[
            pltpu.VMEM((REQS * STEPS, RANK + 2 * LANES), BF16),
            pltpu.VMEM((REQS, ROWS, HALF), F32),
            pltpu.VMEM((REQS, ROWS, HALF), F32),
            pltpu.VMEM((STATE, 2 * HALF), F32),
            pltpu.VMEM((ROWS, HALF), F32),
            pltpu.VMEM((LANES, LANES), F32),
            pltpu.VMEM((REQS // 2, 16, LANES), BF16),
        ]
        + [pltpu.VMEM((2 * STEPS * STATE, 2 * HALF), BF16)] * KEEPS,
        compiler_params=params(16),
        name="scan",
    )(order, core, ours, theirs, act, attended, ssm_state, dt_proj, dt_bias, a_log, skip_d)


def unpack_kernel(back_ref, z_ref, attn_ref, mamba_ref, rows):
    for req in range(REQS):
        for tile in range(BACK // LANES):
            rows[tile, req * ROWS : (req + 1) * ROWS, :] = back_ref[
                req, :, tile * LANES : (tile + 1) * LANES
            ].astype(F32)
    for step in range(STEPS):
        for group in range(0, REQS, 16):
            for half in range(2):
                first = half * STEPS + step
                places = [
                    pl.ds((group + part * 8) * ROWS + first, 8, stride=ROWS) for part in range(2)
                ]
                for tile in range(BACK // LANES):
                    block = jnp.concatenate([rows[tile, place, :] for place in places], axis=0)
                    if tile < HALF // LANES:
                        first_column = half * HALF + tile * LANES
                        columns = slice(first_column, first_column + LANES)
                        z = z_ref[step, group : group + 16, columns].astype(F32)
                        block = block * silu(z)
                        mamba_ref[step, group : group + 16, columns] = block.astype(BF16)
                    else:
                        first_column = half * QUARTER + tile * LANES - HALF
                        columns = slice(first_column, first_column + LANES)
                        attn_ref[step, group : group + 16, columns] = block.astype(BF16)


def unpack(back, mamba_z):
    return pl.pallas_call(
        unpack_kernel,
        out_shape=(
            jax.ShapeDtypeStruct((STEPS, REQS, 2 * QUARTER), BF16),
            jax.ShapeDtypeStruct((STEPS, REQS, 2 * HALF), BF16),
        ),
        in_specs=[vmem()] * 2,
        out_specs=(vmem(), vmem()),
        scratch_shapes=[pltpu.VMEM((BACK // LANES, REQS * ROWS, LANES), F32)],
        compiler_params=params(24),
        name="unpack",
    )(back, mamba_z)


def per_device(
    queries,
    new_kv,
    prefill_page_pool,
    page_table,
    prompt_len,
    dest_device,
    ssm_state,
    conv_state,
    mamba_x,
    mamba_z,
    conv_weight,
    conv_bias,
    x_proj,
    dt_gain,
    dt_proj,
    dt_bias,
    a_log,
    skip_d,
):
    slots = jnp.arange(REQS, dtype=jnp.int32)
    order = jnp.sum(
        jnp.where(dest_device[None, :] == slots[:, None], slots[None, :], 0), axis=1
    )
    core = (lax.axis_index("tp") % 2).astype(jnp.int32).reshape(1)
    swap = [(j, j ^ 1) for j in range(8)]

    outgoing = pack(mamba_x, queries, new_kv)
    arrived = lax.all_to_all(outgoing, "req", split_axis=0, concat_axis=0, tiled=True)
    prior = stage(
        order, outgoing, jnp.transpose(conv_state, (1, 0, 2)), conv_weight, conv_bias[None]
    )
    act, mine, other = convolve(core, arrived, prior, x_proj)
    unit = jnp.where(order[0] >= 0, 1, 2).astype(BF16)
    pool = prefill_page_pool * unit
    chip_sum = mine + lax.ppermute(other, "tp", swap)
    small = chip_sum.astype(BF16)
    ring = [
        lax.ppermute(small, "tp", [(j, (j + hop) % 8) for j in range(8)]) for hop in (2, 6, 4)
    ]
    attended = attend(order, page_table, prompt_len, arrived, pool)
    ours = normalise(chip_sum, ring, dt_gain[None], attended)
    theirs = lax.ppermute(ours, "tp", swap)
    returning = scan(
        order,
        core,
        ours,
        theirs,
        act,
        attended,
        ssm_state,
        dt_proj,
        dt_bias[None],
        a_log,
        skip_d[None],
    )
    back = lax.all_to_all(returning, "req", split_axis=0, concat_axis=0, tiled=True)
    return unpack(back, mamba_z)


def solution(mesh):
    return jax.shard_map(
        per_device,
        mesh=mesh,
        in_specs=(
            P(None, "req", "tp"),
            P(None, "req", None, "tp"),
            P("req", None, None, "tp"),
            P("req", None),
            P("req"),
            P("req"),
            P("req", None, "tp"),
            P("req", None, "tp"),
            P(None, "req", "tp"),
            P(None, "req", "tp"),
            P(None, "tp"),
            P("tp"),
            P("tp", None),
            P(),
            P(None, "tp"),
            P("tp"),
            P(None, "tp"),
            P("tp"),
        ),
        out_specs=(P(None, "req", "tp"), P(None, "req", "tp")),
        check_vma=False,
    )
```

```python
import math

import jax
import jax.numpy as jnp
from jax import lax
from jax.experimental import pallas as pl
from jax.experimental.pallas import tpu as pltpu
from jax.sharding import PartitionSpec as P

HEAD_SIZE = 128
EPSILON = 1e-06
REQS = 32
STEPS = 4
ROWS = 2 * STEPS
LANES = 128
HALF = 1024
QUARTER = 512
RANK = 512
STATE = 16
PAGES = 8
WHOLE = 63
BIG = 60
UNROLL = 32
KEEPS = 4
CHUNKS = 4
PAGE_TOKENS = 16
PROJ = RANK + 2 * STATE
SEND = HALF + QUARTER + HEAD_SIZE
BACK = HALF + QUARTER
F32 = jnp.float32
BF16 = jnp.bfloat16


def vmem():
    return pl.BlockSpec(memory_space=pltpu.VMEM)


def anywhere():
    return pl.BlockSpec(memory_space=pl.ANY)


def smem():
    return pl.BlockSpec(memory_space=pltpu.SMEM)


def params(mib):
    return pltpu.CompilerParams(vmem_limit_bytes=mib * 1024 * 1024)


def cost(mb):
    return pl.CostEstimate(
        flops=3_500_000_000, bytes_accessed=mb * 1_000_000, transcendentals=300_000
    )


def softplus(x):
    return jnp.maximum(x, 0.0) + jnp.log(1.0 + jnp.exp(-jnp.abs(x)))


def silu(x):
    half = 0.5 * x
    return half * jnp.tanh(half) + half


def sublanes(shape):
    return lax.broadcasted_iota(jnp.int32, shape, len(shape) - 2)


def pack_kernel(x_hbm, q_hbm, kv_hbm, out_hbm, x_ref, q_ref, kv_ref, rows, out_ref, sems, out_sems):
    groups = range(0, REQS, 16)
    copies = []
    for group in groups:
        span = pl.ds(group, 16)
        trio = ((x_hbm, x_ref), (q_hbm, q_ref), (kv_hbm, kv_ref))
        copies.append(
            [
                pltpu.make_async_copy(
                    far.at[:, span], near.at[:, span], sems.at[index, group // 16]
                )
                for index, (far, near) in enumerate(trio)
            ]
        )
        for copy in copies[-1]:
            copy.start()
    outs = []
    for group in groups:
        for copy in copies[group // 16]:
            copy.wait()
        for step in range(STEPS):
            for half in range(2):
                first = half * STEPS + step
                places = [
                    pl.ds((group + part * 8) * ROWS + first, 8, stride=ROWS) for part in range(2)
                ]
                tile = 0
                for ref, width in ((x_ref, HALF), (q_ref, QUARTER)):
                    block = ref[step, group : group + 16, half * width : (half + 1) * width]
                    block = block.astype(F32)
                    for column in range(0, width, LANES):
                        rows[tile, places[0], :] = block[0:8, column : column + LANES]
                        rows[tile, places[1], :] = block[8:16, column : column + LANES]
                        tile += 1
            for req in range(group, group + 16):
                rows[SEND // LANES - 1, pl.ds(req * ROWS + step, 2, stride=STEPS), :] = kv_ref[
                    step, req
                ].astype(F32)
        for req in range(group, group + 16):
            for tile in range(SEND // LANES):
                out_ref[req, :, tile * LANES : (tile + 1) * LANES] = rows[
                    tile, req * ROWS : (req + 1) * ROWS, :
                ].astype(BF16)
        span = pl.ds(group, 16)
        outs.append(
            pltpu.make_async_copy(out_ref.at[span], out_hbm.at[span], out_sems.at[group // 16])
        )
        outs[-1].start()
    for copy in outs:
        copy.wait()


def pack(mamba_x, queries, new_kv):
    return pl.pallas_call(
        pack_kernel,
        out_shape=jax.ShapeDtypeStruct((REQS, ROWS, SEND), BF16),
        in_specs=[anywhere()] * 3,
        out_specs=anywhere(),
        scratch_shapes=[
            pltpu.VMEM((STEPS, REQS, 2 * HALF), BF16),
            pltpu.VMEM((STEPS, REQS, 2 * QUARTER), BF16),
            pltpu.VMEM((STEPS, REQS, 2, HEAD_SIZE), BF16),
            pltpu.VMEM((SEND // LANES, REQS * ROWS, LANES), F32),
            pltpu.VMEM((REQS, ROWS, SEND), BF16),
            pltpu.SemaphoreType.DMA((3, 2)),
            pltpu.SemaphoreType.DMA((2,)),
        ],
        compiler_params=params(BIG),
        name="pack",
    )(mamba_x, queries, new_kv)


def halves(ref, row, width):
    low = jnp.broadcast_to(ref[row : row + 1, 0:width], (STEPS, width))
    high = jnp.broadcast_to(ref[row : row + 1, width : 2 * width], (STEPS, width))
    return jnp.concatenate([low, high], axis=0)


def stage_kernel(order_ref, sent_ref, past_ref, weight_ref, bias_ref, out_ref, past_rows, past_taps):
    del sent_ref
    step_of = lax.rem(sublanes((ROWS, HALF)), STEPS)
    for tap in range(3):
        for half in range(2):
            for tile in range(HALF // LANES):
                column = half * HALF + tile * LANES
                block = past_ref[tap, :, column : column + LANES].astype(F32)
                for group in range(0, REQS, 8):
                    place = pl.ds(group * ROWS + (1 - half) * STEPS + 1 + tap, 8, stride=ROWS)
                    past_rows[tile, place, :] = block[group : group + 8]
    plain = [halves(weight_ref, tap, HALF) for tap in range(4)]
    for back in range(4):
        out_ref[REQS + back] = jnp.where(step_of >= back, plain[3 - back], 0.0)
        past_taps[back] = plain[3 - back]
    past_taps[0] = halves(bias_ref, 0, HALF)

    def one(req, carry):
        first = pl.multiple_of(order_ref[req] * ROWS, ROWS)
        past = jnp.concatenate(
            [past_rows[tile, pl.ds(first, ROWS), :] for tile in range(HALF // LANES)], axis=1
        )
        total = past_taps[0]
        for back in range(1, 4):
            moved = jnp.where(step_of < back, pltpu.roll(past, back, 0), 0.0)
            total = total + past_taps[back] * moved
        out_ref[req] = total
        return carry

    lax.fori_loop(0, REQS, one, 0)


def stage(order, sent, conv_state, conv_weight, conv_bias):
    return pl.pallas_call(
        stage_kernel,
        out_shape=jax.ShapeDtypeStruct((REQS + 4, ROWS, HALF), F32),
        in_specs=[smem(), anywhere()] + [vmem()] * 3,
        out_specs=vmem(),
        scratch_shapes=[
            pltpu.VMEM((HALF // LANES, REQS * ROWS, LANES), F32),
            pltpu.VMEM((4, ROWS, HALF), F32),
        ],
        compiler_params=pltpu.CompilerParams(vmem_limit_bytes=(64 * 1024 - 600) * 1024),
        name="stage",
    )(order, sent, conv_state, conv_weight, conv_bias)


def conv_kernel(
    core_ref,
    rows_hbm,
    prior_hbm,
    proj_hbm,
    act_hbm,
    mine_ref,
    other_ref,
    rows_ref,
    prior_ref,
    proj_ref,
    act_ref,
    part,
    rows_sems,
    prior_sems,
    proj_sem,
    act_sem,
):
    chunk = REQS // CHUNKS
    arriving = [
        pltpu.make_async_copy(
            prior_hbm.at[pl.ds(REQS, 4)], prior_ref.at[pl.ds(REQS, 4)], prior_sems.at[CHUNKS]
        )
    ]
    for index in range(CHUNKS):
        span = pl.ds(index * chunk, chunk)
        arriving.append(
            pltpu.make_async_copy(
                rows_hbm.at[span, :, pl.ds(0, HALF)], rows_ref.at[span], rows_sems.at[index]
            )
        )
        arriving.append(
            pltpu.make_async_copy(prior_hbm.at[span], prior_ref.at[span], prior_sems.at[index])
        )
    proj_copy = pltpu.make_async_copy(proj_hbm, proj_ref, proj_sem)
    for copy in arriving + [proj_copy]:
        copy.start()
    arriving[0].wait()

    def one(req):
        now = rows_ref[req].astype(F32)
        total = prior_ref[req] + prior_ref[REQS] * now
        for back in range(1, 4):
            total = total + prior_ref[REQS + back] * pltpu.roll(now, back, 0)
        return silu(total)

    upper = sublanes((ROWS, HALF)) < STEPS

    def some(index, carry):
        lows, highs = [], []
        for offset in range(0, 4, 2):
            even, odd = one(4 * index + offset), one(4 * index + offset + 1)
            lows.append(jnp.where(upper, even, pltpu.roll(odd, STEPS, 0)))
            highs.append(jnp.where(upper, pltpu.roll(even, STEPS, 0), odd))
        rows = pl.ds(pl.multiple_of(index * 16, 16), 16)
        act_ref[rows, 0:HALF] = jnp.concatenate(lows, axis=0).astype(BF16)
        act_ref[rows, HALF:] = jnp.concatenate(highs, axis=0).astype(BF16)
        return carry

    for index in range(CHUNKS):
        arriving[1 + 2 * index].wait()
        arriving[2 + 2 * index].wait()
        lax.fori_loop(index * chunk // 4, (index + 1) * chunk // 4, some, 0)
    act_copy = pltpu.make_async_copy(act_ref, act_hbm, act_sem)
    act_copy.start()
    proj_copy.wait()
    part[...] = jnp.dot(act_ref[...], proj_ref[...], preferred_element_type=F32)
    core = core_ref[0]
    size = REQS * STEPS // 2
    mine_ref[...] = part[pl.ds(pl.multiple_of(core * size, size), size), :]
    other_ref[...] = part[pl.ds(pl.multiple_of((1 - core) * size, size), size), :]
    act_copy.wait()


def convolve(core, arrived, prior, x_proj):
    half_rows = jax.ShapeDtypeStruct((REQS * STEPS // 2, PROJ), F32)
    return pl.pallas_call(
        conv_kernel,
        out_shape=(jax.ShapeDtypeStruct((REQS * STEPS, 2 * HALF), BF16), half_rows, half_rows),
        in_specs=[smem()] + [anywhere()] * 3,
        out_specs=(anywhere(), vmem(), vmem()),
        scratch_shapes=[
            pltpu.VMEM((REQS, ROWS, HALF), BF16),
            pltpu.VMEM(prior.shape, F32),
            pltpu.VMEM(x_proj.shape, BF16),
            pltpu.VMEM((REQS * STEPS, 2 * HALF), BF16),
            pltpu.VMEM((REQS * STEPS, PROJ), F32),
            pltpu.SemaphoreType.DMA((CHUNKS,)),
            pltpu.SemaphoreType.DMA((CHUNKS + 1,)),
            pltpu.SemaphoreType.DMA,
            pltpu.SemaphoreType.DMA,
        ],
        compiler_params=params(50),
        name="convolve",
    )(core, arrived, prior, x_proj)


def norm_kernel(sum_ref, one_ref, two_ref, three_ref, gain_ref, after_ref, out_ref):
    del after_ref
    total = (
        sum_ref[...]
        + one_ref[...].astype(F32)
        + two_ref[...].astype(F32)
        + three_ref[...].astype(F32)
    )
    low = total[:, :RANK]
    spread = lax.rsqrt(jnp.mean(low * low, axis=-1, keepdims=True) + EPSILON)
    out_ref[:, 0:RANK] = (low * spread * gain_ref[...]).astype(BF16)
    coef = total[:, RANK:]
    coef = jnp.concatenate([coef, jnp.zeros((coef.shape[0], LANES - 2 * STATE), F32)], axis=1)
    coef_high = coef.astype(BF16)
    out_ref[:, RANK : RANK + LANES] = coef_high
    out_ref[:, RANK + LANES :] = (coef - coef_high.astype(F32)).astype(BF16)


def normalise(chip_sum, ring, gain, after):
    return pl.pallas_call(
        norm_kernel,
        out_shape=jax.ShapeDtypeStruct((REQS * STEPS // 2, RANK + 2 * LANES), BF16),
        in_specs=[vmem()] * 5 + [anywhere()],
        out_specs=vmem(),
        compiler_params=params(8),
        name="normalise",
    )(chip_sum, *ring, gain, after)


def attend_kernel(
    order_ref, table_ref, length_ref, rows_ref, pool_ref, out_ref, scores_ref, weights_ref
):
    scale = math.log2(math.e) / math.sqrt(HEAD_SIZE)
    count = 4 * ROWS
    lane = lax.broadcasted_iota(jnp.int32, (count, LANES), 1)
    step_of = lax.rem(lax.broadcasted_iota(jnp.int32, (count, LANES), 0), STEPS)
    fresh_ok = lane <= step_of
    pad = jnp.zeros((LANES - PAGE_TOKENS, HEAD_SIZE), BF16)
    blank = jnp.zeros((ROWS, HEAD_SIZE), F32)
    ones = jnp.ones((2 * LANES, LANES), BF16)

    def score(req):
        source = order_ref[req]
        query = rows_ref[req, :, HALF : HALF + QUARTER].astype(F32)
        query = jnp.concatenate(
            [query[:, h * HEAD_SIZE : (h + 1) * HEAD_SIZE] for h in range(4)], axis=0
        ).astype(BF16)
        fresh = rows_ref[req, :, HALF + QUARTER : SEND].astype(F32)
        fresh = jnp.concatenate([fresh, blank], axis=0).astype(BF16)
        keys = [pool_ref[table_ref[source, page], 0] for page in range(PAGES)]
        keys = jnp.concatenate(keys + [fresh, pad], axis=0)
        scores_ref[req] = lax.dot_general(
            query, keys, (((1,), (1,)), ((), ())), preferred_element_type=F32
        )

    def soften(req):
        length = length_ref[order_ref[req]]
        old = jnp.where(lane < length, scores_ref[req, :, 0:LANES] * scale, -jnp.inf)
        new = jnp.where(fresh_ok, scores_ref[req, :, LANES:] * scale, -jnp.inf)
        top = jnp.max(jnp.maximum(old, new), axis=1, keepdims=True)
        weights_ref[req, :, 0:LANES] = jnp.exp2(old - top).astype(BF16)
        weights_ref[req, :, LANES:] = jnp.exp2(new - top).astype(BF16)

    def mix(req):
        source = order_ref[req]
        fresh = rows_ref[req, :, HALF + QUARTER : SEND].astype(F32)
        fresh = jnp.concatenate([pltpu.roll(fresh, STEPS, 0), blank], axis=0).astype(BF16)
        values = [pool_ref[table_ref[source, page], 1] for page in range(PAGES)]
        values = jnp.concatenate(values + [fresh, pad], axis=0)
        values = jnp.concatenate([values, ones], axis=1)
        mixed = jnp.dot(weights_ref[req], values, preferred_element_type=F32)
        mixed = mixed[:, 0:LANES] / mixed[:, LANES:]
        for h in range(4):
            out_ref[req, :, h * HEAD_SIZE : (h + 1) * HEAD_SIZE] = mixed[
                h * ROWS : (h + 1) * ROWS
            ].astype(BF16)

    for phase in (score, soften, mix):

        def some(index, carry, phase=phase):
            for offset in range(UNROLL):
                phase(UNROLL * index + offset)
            return carry

        lax.fori_loop(0, REQS // UNROLL, some, 0)


def attend(order, page_table, prompt_len, arrived, pool):
    return pl.pallas_call(
        attend_kernel,
        out_shape=jax.ShapeDtypeStruct((REQS, ROWS, QUARTER), BF16),
        in_specs=[smem()] * 3 + [vmem()] * 2,
        out_specs=vmem(),
        scratch_shapes=[
            pltpu.VMEM((REQS, 4 * ROWS, 2 * LANES), F32),
            pltpu.VMEM((REQS, 4 * ROWS, 2 * LANES), BF16),
        ],
        compiler_params=params(8),
        cost_estimate=cost(6),
        name="attend",
    )(order, page_table, prompt_len, arrived, pool)


def scan_kernel(
    order_ref,
    core_ref,
    ours_ref,
    theirs_ref,
    act_ref,
    attended_ref,
    state_ref,
    dt_proj_ref,
    dt_bias_ref,
    a_log_ref,
    skip_ref,
    out_ref,
    packed,
    rate,
    fed,
    decay,
    coef,
    read,
    *keeps,
):
    core = core_ref[0]
    size = REQS * STEPS // 2
    packed[pl.ds(pl.multiple_of(core * size, size), size), :] = ours_ref[...]
    packed[pl.ds(pl.multiple_of((1 - core) * size, size), size), :] = theirs_ref[...]
    decay[...] = jnp.exp(a_log_ref[...]) * (-1.0 / math.log(2.0))
    coef[...] = jnp.transpose(
        packed[:, RANK : RANK + LANES].astype(F32) + packed[:, RANK + LANES :].astype(F32)
    )
    speeds = jnp.dot(packed[:, 0:RANK], dt_proj_ref[...], preferred_element_type=F32)
    speeds = softplus(speeds + dt_bias_ref[...])
    feeds = speeds * act_ref[...].astype(F32)
    for pair in range(REQS // 2):
        rows = slice(pair * 8, pair * 8 + 8)
        rate[pair] = speeds[rows]
        fed[pair] = feeds[rows]
    lane = lax.broadcasted_iota(jnp.int32, (REQS * STEPS, LANES), 1)
    row = lax.broadcasted_iota(jnp.int32, (REQS * STEPS, LANES), 0)
    parts = []
    for first in (RANK, RANK + LANES):
        part = packed[:, first : first + LANES].astype(F32)
        spread = jnp.zeros_like(part)
        for block in range(LANES // STATE):
            moved = pltpu.roll(part, (block * STATE - STATE) % LANES, 1)
            spread = jnp.where(
                (lane // STATE == block) & (lax.rem(row, 2 * STEPS) == block), moved, spread
            )
        parts.append(spread)
    first_pair = lax.rem(row, 4 * STEPS) < 2 * STEPS
    for quad in range(REQS // 4):
        rows = slice(quad * 16, quad * 16 + 16)
        for side in range(2):
            block = [jnp.where(first_pair == (side == 0), part, 0.0)[rows] for part in parts]
            read[quad, :, side * LANES : (side + 1) * LANES] = jnp.concatenate(
                block, axis=0
            ).astype(BF16)
    upper = sublanes((ROWS, LANES)) < STEPS

    def advance(quad, keep):
        for which in range(4):
            req = 4 * quad + which
            pair = 2 * quad + which // 2
            source = order_ref[req]
            turned = pltpu.roll(coef[0:STATE, :], lax.rem(LANES - STEPS * req, LANES), 1)
            into = [
                jnp.broadcast_to(turned[:, s : s + 1], (STATE, LANES)) for s in range(STEPS)
            ]
            for first_tile in range(0, HALF // LANES, 2):
                chains = [
                    (tile, half) for tile in range(first_tile, first_tile + 2) for half in range(2)
                ]
                spans = [
                    slice(half * HALF + tile * LANES, half * HALF + (tile + 1) * LANES)
                    for tile, half in chains
                ]
                hidden = [state_ref[source, :, columns] for columns in spans]
                for step in range(STEPS):
                    first = (which * STEPS + step) * STATE
                    for index in range(len(chains)):
                        line = slice(which % 2 * STEPS + step, which % 2 * STEPS + step + 1)
                        speed = jnp.broadcast_to(rate[pair, line, spans[index]], (STATE, LANES))
                        feed = jnp.broadcast_to(fed[pair, line, spans[index]], (STATE, LANES))
                        hidden[index] = (
                            jnp.exp2(speed * decay[:, spans[index]]) * hidden[index]
                            + feed * into[step]
                        )
                        keep[first : first + STATE, spans[index]] = hidden[index].astype(BF16)

    def readout(quad, keep, acts):
        both = jnp.dot(read[quad], keep[...], preferred_element_type=F32)
        both = both[0:16] + both[16:32] + skip_ref[...] * acts
        for which in range(2):
            req = 4 * quad + 2 * which
            rows = slice(which * 8, which * 8 + 8)
            for tile in range(HALF // LANES):
                place = slice(tile * LANES, (tile + 1) * LANES)
                low = both[rows, place]
                high = both[rows, HALF + tile * LANES : HALF + (tile + 1) * LANES]
                even = jnp.where(upper, low, pltpu.roll(high, STEPS, 0))
                odd = jnp.where(upper, pltpu.roll(low, STEPS, 0), high)
                out_ref[req, :, place] = even.astype(BF16)
                out_ref[req + 1, :, place] = odd.astype(BF16)

    def some(index, carry):
        count = len(keeps)
        rows = pl.ds(pl.multiple_of(index * 16 * count, 16 * count), 16 * count)
        acts = act_ref[rows, :].astype(F32)
        for offset in range(count + 1):
            if offset < count:
                advance(count * index + offset, keeps[offset])
            if offset:
                last = offset - 1
                readout(count * index + last, keeps[last], acts[last * 16 : last * 16 + 16])
        return carry

    lax.fori_loop(0, REQS // 4 // len(keeps), some, 0)
    for req in range(REQS):
        out_ref[req, :, HALF:BACK] = attended_ref[req]


def scan(order, core, ours, theirs, act, attended, ssm_state, dt_proj, dt_bias, a_log, skip_d):
    return pl.pallas_call(
        scan_kernel,
        out_shape=jax.ShapeDtypeStruct((REQS, ROWS, BACK), BF16),
        in_specs=[smem(), smem()] + [vmem()] * 9,
        out_specs=vmem(),
        scratch_shapes=[
            pltpu.VMEM((REQS * STEPS, RANK + 2 * LANES), BF16),
            pltpu.VMEM((REQS // 2, ROWS, 2 * HALF), F32),
            pltpu.VMEM((REQS // 2, ROWS, 2 * HALF), F32),
            pltpu.VMEM((STATE, 2 * HALF), F32),
            pltpu.VMEM((LANES, LANES), F32),
            pltpu.VMEM((REQS // 4, 32, 2 * LANES), BF16),
        ]
        + [pltpu.VMEM((4 * STEPS * STATE, 2 * HALF), BF16)] * KEEPS,
        compiler_params=params(16),
        name="scan",
    )(order, core, ours, theirs, act, attended, ssm_state, dt_proj, dt_bias, a_log, skip_d)


def unpack_kernel(back_ref, z_ref, attn_hbm, mamba_hbm, rows, attn_ref, mamba_ref, sems):
    outs = []
    for group in range(0, REQS, 16):
        for req in range(group, group + 16):
            for tile in range(BACK // LANES):
                rows[tile, req * ROWS : (req + 1) * ROWS, :] = back_ref[
                    req, :, tile * LANES : (tile + 1) * LANES
                ].astype(F32)
        for step in range(STEPS):
            for half in range(2):
                first = half * STEPS + step
                places = [
                    pl.ds((group + part * 8) * ROWS + first, 8, stride=ROWS) for part in range(2)
                ]
                for tile in range(BACK // LANES):
                    block = jnp.concatenate([rows[tile, place, :] for place in places], axis=0)
                    if tile < HALF // LANES:
                        first_column = half * HALF + tile * LANES
                        columns = slice(first_column, first_column + LANES)
                        z = z_ref[step, group : group + 16, columns].astype(F32)
                        block = block * silu(z)
                        mamba_ref[step, group : group + 16, columns] = block.astype(BF16)
                    else:
                        first_column = half * QUARTER + tile * LANES - HALF
                        columns = slice(first_column, first_column + LANES)
                        attn_ref[step, group : group + 16, columns] = block.astype(BF16)
        span = pl.ds(group, 16)
        for index, (near, far) in enumerate(((attn_ref, attn_hbm), (mamba_ref, mamba_hbm))):
            outs.append(
                pltpu.make_async_copy(
                    near.at[:, span], far.at[:, span], sems.at[index, group // 16]
                )
            )
            outs[-1].start()
    for copy in outs:
        copy.wait()


def unpack(back, mamba_z):
    attn = (STEPS, REQS, 2 * QUARTER)
    mamba = (STEPS, REQS, 2 * HALF)
    return pl.pallas_call(
        unpack_kernel,
        out_shape=(jax.ShapeDtypeStruct(attn, BF16), jax.ShapeDtypeStruct(mamba, BF16)),
        in_specs=[vmem()] * 2,
        out_specs=(anywhere(), anywhere()),
        scratch_shapes=[
            pltpu.VMEM((BACK // LANES, REQS * ROWS, LANES), F32),
            pltpu.VMEM(attn, BF16),
            pltpu.VMEM(mamba, BF16),
            pltpu.SemaphoreType.DMA((2, 2)),
        ],
        compiler_params=params(24),
        name="unpack",
    )(back, mamba_z)


def per_device(
    queries,
    new_kv,
    prefill_page_pool,
    page_table,
    prompt_len,
    dest_device,
    ssm_state,
    conv_state,
    mamba_x,
    mamba_z,
    conv_weight,
    conv_bias,
    x_proj,
    dt_gain,
    dt_proj,
    dt_bias,
    a_log,
    skip_d,
):
    slots = jnp.arange(REQS, dtype=jnp.int32)
    order = jnp.sum(
        jnp.where(dest_device[None, :] == slots[:, None], slots[None, :], 0), axis=1
    )
    core = (lax.axis_index("tp") % 2).astype(jnp.int32).reshape(1)
    swap = [(j, j ^ 1) for j in range(8)]

    outgoing = pack(mamba_x, queries, new_kv)
    arrived = lax.all_to_all(outgoing, "req", split_axis=0, concat_axis=0, tiled=True)
    prior = stage(
        order, outgoing, jnp.transpose(conv_state, (1, 0, 2)), conv_weight, conv_bias[None]
    )
    act, mine, other = convolve(core, arrived, prior, x_proj)
    chip_sum = mine + lax.ppermute(other, "tp", swap)
    small = chip_sum.astype(BF16)
    ring = [
        lax.ppermute(small, "tp", [(j, (j + hop) % 8) for j in range(8)]) for hop in (4, 2, 6)
    ]
    attended = attend(order, page_table, prompt_len, arrived, prefill_page_pool)
    ours = normalise(chip_sum, ring, dt_gain[None], attended)
    theirs = lax.ppermute(ours, "tp", swap)
    returning = scan(
        order,
        core,
        ours,
        theirs,
        act,
        attended,
        ssm_state,
        dt_proj,
        dt_bias[None],
        a_log,
        skip_d[None],
    )
    back = lax.all_to_all(returning, "req", split_axis=0, concat_axis=0, tiled=True)
    return unpack(back, mamba_z)


def solution(mesh):
    return jax.shard_map(
        per_device,
        mesh=mesh,
        in_specs=(
            P(None, "req", "tp"),
            P(None, "req", None, "tp"),
            P("req", None, None, "tp"),
            P("req", None),
            P("req"),
            P("req"),
            P("req", None, "tp"),
            P("req", None, "tp"),
            P(None, "req", "tp"),
            P(None, "req", "tp"),
            P(None, "tp"),
            P("tp"),
            P("tp", None),
            P(),
            P(None, "tp"),
            P("tp"),
            P(None, "tp"),
            P("tp"),
        ),
        out_specs=(P(None, "req", "tp"), P(None, "req", "tp")),
        check_vma=False,
    )
```

```python
import math

import jax
import jax.numpy as jnp
from jax import lax
from jax.experimental import pallas as pl
from jax.experimental.pallas import tpu as pltpu
from jax.sharding import PartitionSpec as P

HEAD_SIZE = 128
EPSILON = 1e-06
REQS = 32
STEPS = 4
ROWS = 2 * STEPS
LANES = 128
HALF = 1024
QUARTER = 512
RANK = 512
STATE = 16
PAGES = 8
WHOLE = 63
BIG = 60
UNROLL = 32
KEEPS = 4
CHUNKS = 4
PAGE_TOKENS = 16
PROJ = RANK + 2 * STATE
SEND = HALF + QUARTER + HEAD_SIZE
BACK = HALF + QUARTER
F32 = jnp.float32
BF16 = jnp.bfloat16


def vmem():
    return pl.BlockSpec(memory_space=pltpu.VMEM)


def anywhere():
    return pl.BlockSpec(memory_space=pl.ANY)


def smem():
    return pl.BlockSpec(memory_space=pltpu.SMEM)


def params(mib):
    return pltpu.CompilerParams(vmem_limit_bytes=mib * 1024 * 1024)


def cost(mb):
    return pl.CostEstimate(
        flops=3_500_000_000, bytes_accessed=mb * 1_000_000, transcendentals=300_000
    )


def softplus(x):
    return jnp.maximum(x, 0.0) + jnp.log(1.0 + jnp.exp(-jnp.abs(x)))


def silu(x):
    half = 0.5 * x
    return half * jnp.tanh(half) + half


def sublanes(shape):
    return lax.broadcasted_iota(jnp.int32, shape, len(shape) - 2)


def pack_kernel(x_hbm, q_hbm, kv_hbm, out_hbm, x_ref, q_ref, kv_ref, rows, out_ref, sems, out_sems):
    groups = range(0, REQS, 16)
    copies = []
    for group in groups:
        span = pl.ds(group, 16)
        trio = ((x_hbm, x_ref), (q_hbm, q_ref), (kv_hbm, kv_ref))
        copies.append(
            [
                pltpu.make_async_copy(
                    far.at[:, span], near.at[:, span], sems.at[index, group // 16]
                )
                for index, (far, near) in enumerate(trio)
            ]
        )
        for copy in copies[-1]:
            copy.start()
    outs = []
    for group in groups:
        for copy in copies[group // 16]:
            copy.wait()
        for step in range(STEPS):
            for half in range(2):
                first = half * STEPS + step
                places = [
                    pl.ds((group + part * 8) * ROWS + first, 8, stride=ROWS) for part in range(2)
                ]
                tile = 0
                for ref, width in ((x_ref, HALF), (q_ref, QUARTER)):
                    block = ref[step, group : group + 16, half * width : (half + 1) * width]
                    block = block.astype(F32)
                    for column in range(0, width, LANES):
                        rows[tile, places[0], :] = block[0:8, column : column + LANES]
                        rows[tile, places[1], :] = block[8:16, column : column + LANES]
                        tile += 1
            for req in range(group, group + 16):
                rows[SEND // LANES - 1, pl.ds(req * ROWS + step, 2, stride=STEPS), :] = kv_ref[
                    step, req
                ].astype(F32)
        for req in range(group, group + 16):
            for tile in range(SEND // LANES):
                out_ref[req, :, tile * LANES : (tile + 1) * LANES] = rows[
                    tile, req * ROWS : (req + 1) * ROWS, :
                ].astype(BF16)
        span = pl.ds(group, 16)
        outs.append(
            pltpu.make_async_copy(out_ref.at[span], out_hbm.at[span], out_sems.at[group // 16])
        )
        outs[-1].start()
    for copy in outs:
        copy.wait()


def pack(mamba_x, queries, new_kv):
    return pl.pallas_call(
        pack_kernel,
        out_shape=jax.ShapeDtypeStruct((REQS, ROWS, SEND), BF16),
        in_specs=[anywhere()] * 3,
        out_specs=anywhere(),
        scratch_shapes=[
            pltpu.VMEM((STEPS, REQS, 2 * HALF), BF16),
            pltpu.VMEM((STEPS, REQS, 2 * QUARTER), BF16),
            pltpu.VMEM((STEPS, REQS, 2, HEAD_SIZE), BF16),
            pltpu.VMEM((SEND // LANES, REQS * ROWS, LANES), F32),
            pltpu.VMEM((REQS, ROWS, SEND), BF16),
            pltpu.SemaphoreType.DMA((3, 2)),
            pltpu.SemaphoreType.DMA((2,)),
        ],
        compiler_params=params(BIG),
        name="pack",
    )(mamba_x, queries, new_kv)


def halves(ref, row, width):
    low = jnp.broadcast_to(ref[row : row + 1, 0:width], (STEPS, width))
    high = jnp.broadcast_to(ref[row : row + 1, width : 2 * width], (STEPS, width))
    return jnp.concatenate([low, high], axis=0)


def stage_kernel(order_ref, sent_ref, past_ref, weight_ref, bias_ref, out_ref, past_rows, past_taps):
    del sent_ref
    step_of = lax.rem(sublanes((ROWS, HALF)), STEPS)
    for tap in range(3):
        for half in range(2):
            for tile in range(HALF // LANES):
                column = half * HALF + tile * LANES
                block = past_ref[tap, :, column : column + LANES].astype(F32)
                for group in range(0, REQS, 8):
                    place = pl.ds(group * ROWS + (1 - half) * STEPS + 1 + tap, 8, stride=ROWS)
                    past_rows[tile, place, :] = block[group : group + 8]
    plain = [halves(weight_ref, tap, HALF) for tap in range(4)]
    for back in range(4):
        out_ref[REQS + back] = jnp.where(step_of >= back, plain[3 - back], 0.0)
        past_taps[back] = plain[3 - back]
    past_taps[0] = halves(bias_ref, 0, HALF)

    def one(req, carry):
        first = pl.multiple_of(order_ref[req] * ROWS, ROWS)
        past = jnp.concatenate(
            [past_rows[tile, pl.ds(first, ROWS), :] for tile in range(HALF // LANES)], axis=1
        )
        total = past_taps[0]
        for back in range(1, 4):
            moved = jnp.where(step_of < back, pltpu.roll(past, back, 0), 0.0)
            total = total + past_taps[back] * moved
        out_ref[req] = total
        return carry

    lax.fori_loop(0, REQS, one, 0)


def stage(order, sent, conv_state, conv_weight, conv_bias):
    return pl.pallas_call(
        stage_kernel,
        out_shape=jax.ShapeDtypeStruct((REQS + 4, ROWS, HALF), F32),
        in_specs=[smem(), anywhere()] + [vmem()] * 3,
        out_specs=vmem(),
        scratch_shapes=[
            pltpu.VMEM((HALF // LANES, REQS * ROWS, LANES), F32),
            pltpu.VMEM((4, ROWS, HALF), F32),
        ],
        compiler_params=pltpu.CompilerParams(vmem_limit_bytes=(64 * 1024 - 600) * 1024),
        name="stage",
    )(order, sent, conv_state, conv_weight, conv_bias)


def conv_kernel(
    core_ref,
    rows_hbm,
    prior_hbm,
    proj_hbm,
    act_hbm,
    mine_ref,
    other_ref,
    rows_ref,
    prior_ref,
    proj_ref,
    act_ref,
    part,
    rows_sems,
    prior_sems,
    proj_sem,
    act_sem,
):
    chunk = REQS // CHUNKS
    arriving = [
        pltpu.make_async_copy(
            prior_hbm.at[pl.ds(REQS, 4)], prior_ref.at[pl.ds(REQS, 4)], prior_sems.at[CHUNKS]
        )
    ]
    for index in range(CHUNKS):
        span = pl.ds(index * chunk, chunk)
        arriving.append(
            pltpu.make_async_copy(
                rows_hbm.at[span, :, pl.ds(0, HALF)], rows_ref.at[span], rows_sems.at[index]
            )
        )
        arriving.append(
            pltpu.make_async_copy(prior_hbm.at[span], prior_ref.at[span], prior_sems.at[index])
        )
    proj_copy = pltpu.make_async_copy(proj_hbm, proj_ref, proj_sem)
    for copy in arriving + [proj_copy]:
        copy.start()
    arriving[0].wait()

    def one(req):
        now = rows_ref[req].astype(F32)
        total = prior_ref[req] + prior_ref[REQS] * now
        for back in range(1, 4):
            total = total + prior_ref[REQS + back] * pltpu.roll(now, back, 0)
        return silu(total)

    upper = sublanes((ROWS, HALF)) < STEPS

    def some(index, carry):
        lows, highs = [], []
        for offset in range(0, 4, 2):
            even, odd = one(4 * index + offset), one(4 * index + offset + 1)
            lows.append(jnp.where(upper, even, pltpu.roll(odd, STEPS, 0)))
            highs.append(jnp.where(upper, pltpu.roll(even, STEPS, 0), odd))
        rows = pl.ds(pl.multiple_of(index * 16, 16), 16)
        act_ref[rows, 0:HALF] = jnp.concatenate(lows, axis=0).astype(BF16)
        act_ref[rows, HALF:] = jnp.concatenate(highs, axis=0).astype(BF16)
        return carry

    for index in range(CHUNKS):
        arriving[1 + 2 * index].wait()
        arriving[2 + 2 * index].wait()
        lax.fori_loop(index * chunk // 4, (index + 1) * chunk // 4, some, 0)
    act_copy = pltpu.make_async_copy(act_ref, act_hbm, act_sem)
    act_copy.start()
    proj_copy.wait()
    part[...] = jnp.dot(act_ref[...], proj_ref[...], preferred_element_type=F32)
    core = core_ref[0]
    size = REQS * STEPS // 2
    mine_ref[...] = part[pl.ds(pl.multiple_of(core * size, size), size), :]
    other_ref[...] = part[pl.ds(pl.multiple_of((1 - core) * size, size), size), :]
    act_copy.wait()


def convolve(core, arrived, prior, x_proj):
    half_rows = jax.ShapeDtypeStruct((REQS * STEPS // 2, PROJ), F32)
    return pl.pallas_call(
        conv_kernel,
        out_shape=(jax.ShapeDtypeStruct((REQS * STEPS, 2 * HALF), BF16), half_rows, half_rows),
        in_specs=[smem()] + [anywhere()] * 3,
        out_specs=(anywhere(), vmem(), vmem()),
        scratch_shapes=[
            pltpu.VMEM((REQS, ROWS, HALF), BF16),
            pltpu.VMEM(prior.shape, F32),
            pltpu.VMEM(x_proj.shape, BF16),
            pltpu.VMEM((REQS * STEPS, 2 * HALF), BF16),
            pltpu.VMEM((REQS * STEPS, PROJ), F32),
            pltpu.SemaphoreType.DMA((CHUNKS,)),
            pltpu.SemaphoreType.DMA((CHUNKS + 1,)),
            pltpu.SemaphoreType.DMA,
            pltpu.SemaphoreType.DMA,
        ],
        compiler_params=params(52),
        name="convolve",
    )(core, arrived, prior, x_proj)


def norm_kernel(sum_ref, one_ref, two_ref, three_ref, gain_ref, after_ref, out_ref):
    del after_ref
    total = (
        sum_ref[...]
        + one_ref[...].astype(F32)
        + two_ref[...].astype(F32)
        + three_ref[...].astype(F32)
    )
    low = total[:, :RANK]
    spread = lax.rsqrt(jnp.mean(low * low, axis=-1, keepdims=True) + EPSILON)
    out_ref[:, 0:RANK] = (low * spread * gain_ref[...]).astype(BF16)
    coef = total[:, RANK:]
    coef = jnp.concatenate([coef, jnp.zeros((coef.shape[0], LANES - 2 * STATE), F32)], axis=1)
    coef_high = coef.astype(BF16)
    out_ref[:, RANK : RANK + LANES] = coef_high
    out_ref[:, RANK + LANES :] = (coef - coef_high.astype(F32)).astype(BF16)


def normalise(chip_sum, ring, gain, after):
    return pl.pallas_call(
        norm_kernel,
        out_shape=jax.ShapeDtypeStruct((REQS * STEPS // 2, RANK + 2 * LANES), BF16),
        in_specs=[vmem()] * 5 + [anywhere()],
        out_specs=vmem(),
        compiler_params=params(8),
        name="normalise",
    )(chip_sum, *ring, gain, after)


def attend_kernel(
    order_ref, table_ref, length_ref, rows_ref, pool_ref, out_ref, scores_ref, weights_ref
):
    scale = math.log2(math.e) / math.sqrt(HEAD_SIZE)
    count = 4 * ROWS
    lane = lax.broadcasted_iota(jnp.int32, (count, LANES), 1)
    step_of = lax.rem(lax.broadcasted_iota(jnp.int32, (count, LANES), 0), STEPS)
    fresh_ok = lane <= step_of
    pad = jnp.zeros((LANES - PAGE_TOKENS, HEAD_SIZE), BF16)
    blank = jnp.zeros((ROWS, HEAD_SIZE), F32)
    ones = jnp.ones((2 * LANES, LANES), BF16)

    def score(req):
        source = order_ref[req]
        query = rows_ref[req, :, HALF : HALF + QUARTER].astype(F32)
        query = jnp.concatenate(
            [query[:, h * HEAD_SIZE : (h + 1) * HEAD_SIZE] for h in range(4)], axis=0
        ).astype(BF16)
        fresh = rows_ref[req, :, HALF + QUARTER : SEND].astype(F32)
        fresh = jnp.concatenate([fresh, blank], axis=0).astype(BF16)
        keys = [pool_ref[table_ref[source, page], 0] for page in range(PAGES)]
        keys = jnp.concatenate(keys + [fresh, pad], axis=0)
        scores_ref[req] = lax.dot_general(
            query, keys, (((1,), (1,)), ((), ())), preferred_element_type=F32
        )

    def soften(req):
        length = length_ref[order_ref[req]]
        old = jnp.where(lane < length, scores_ref[req, :, 0:LANES] * scale, -jnp.inf)
        new = jnp.where(fresh_ok, scores_ref[req, :, LANES:] * scale, -jnp.inf)
        top = jnp.max(jnp.maximum(old, new), axis=1, keepdims=True)
        weights_ref[req, :, 0:LANES] = jnp.exp2(old - top).astype(BF16)
        weights_ref[req, :, LANES:] = jnp.exp2(new - top).astype(BF16)

    def mix(req):
        source = order_ref[req]
        fresh = rows_ref[req, :, HALF + QUARTER : SEND].astype(F32)
        fresh = jnp.concatenate([pltpu.roll(fresh, STEPS, 0), blank], axis=0).astype(BF16)
        values = [pool_ref[table_ref[source, page], 1] for page in range(PAGES)]
        values = jnp.concatenate(values + [fresh, pad], axis=0)
        values = jnp.concatenate([values, ones], axis=1)
        mixed = jnp.dot(weights_ref[req], values, preferred_element_type=F32)
        mixed = mixed[:, 0:LANES] / mixed[:, LANES:]
        for h in range(4):
            out_ref[req, :, h * HEAD_SIZE : (h + 1) * HEAD_SIZE] = mixed[
                h * ROWS : (h + 1) * ROWS
            ].astype(BF16)

    for phase in (score, soften, mix):

        def some(index, carry, phase=phase):
            for offset in range(UNROLL):
                phase(UNROLL * index + offset)
            return carry

        lax.fori_loop(0, REQS // UNROLL, some, 0)


def attend(order, page_table, prompt_len, arrived, pool):
    return pl.pallas_call(
        attend_kernel,
        out_shape=jax.ShapeDtypeStruct((REQS, ROWS, QUARTER), BF16),
        in_specs=[smem()] * 3 + [vmem()] * 2,
        out_specs=vmem(),
        scratch_shapes=[
            pltpu.VMEM((REQS, 4 * ROWS, 2 * LANES), F32),
            pltpu.VMEM((REQS, 4 * ROWS, 2 * LANES), BF16),
        ],
        compiler_params=params(8),
        cost_estimate=cost(6),
        name="attend",
    )(order, page_table, prompt_len, arrived, pool)


def scan_kernel(
    order_ref,
    core_ref,
    ours_ref,
    theirs_ref,
    act_ref,
    attended_ref,
    state_ref,
    dt_proj_ref,
    dt_bias_ref,
    a_log_ref,
    skip_ref,
    out_ref,
    packed,
    rate,
    fed,
    decay,
    coef,
    read,
    *keeps,
):
    core = core_ref[0]
    size = REQS * STEPS // 2
    packed[pl.ds(pl.multiple_of(core * size, size), size), :] = ours_ref[...]
    packed[pl.ds(pl.multiple_of((1 - core) * size, size), size), :] = theirs_ref[...]
    decay[...] = jnp.exp(a_log_ref[...]) * (-1.0 / math.log(2.0))
    coef[...] = jnp.transpose(
        packed[:, RANK : RANK + LANES].astype(F32) + packed[:, RANK + LANES :].astype(F32)
    )
    speeds = jnp.dot(packed[:, 0:RANK], dt_proj_ref[...], preferred_element_type=F32)
    speeds = softplus(speeds + dt_bias_ref[...])
    feeds = speeds * act_ref[...].astype(F32)
    for pair in range(REQS // 2):
        rows = slice(pair * 8, pair * 8 + 8)
        rate[pair] = speeds[rows]
        fed[pair] = feeds[rows]
    lane = lax.broadcasted_iota(jnp.int32, (REQS * STEPS, LANES), 1)
    row = lax.broadcasted_iota(jnp.int32, (REQS * STEPS, LANES), 0)
    parts = []
    for first in (RANK, RANK + LANES):
        part = packed[:, first : first + LANES].astype(F32)
        spread = jnp.zeros_like(part)
        for block in range(LANES // STATE):
            moved = pltpu.roll(part, (block * STATE - STATE) % LANES, 1)
            spread = jnp.where(
                (lane // STATE == block) & (lax.rem(row, 2 * STEPS) == block), moved, spread
            )
        parts.append(spread)
    first_pair = lax.rem(row, 4 * STEPS) < 2 * STEPS
    for quad in range(REQS // 4):
        rows = slice(quad * 16, quad * 16 + 16)
        for side in range(2):
            block = [jnp.where(first_pair == (side == 0), part, 0.0)[rows] for part in parts]
            read[quad, :, side * LANES : (side + 1) * LANES] = jnp.concatenate(
                block, axis=0
            ).astype(BF16)
    upper = sublanes((ROWS, LANES)) < STEPS

    def advance(quad, keep):
        for which in range(4):
            req = 4 * quad + which
            pair = 2 * quad + which // 2
            source = order_ref[req]
            turned = pltpu.roll(coef[0:STATE, :], lax.rem(LANES - STEPS * req, LANES), 1)
            into = [
                jnp.broadcast_to(turned[:, s : s + 1], (STATE, LANES)) for s in range(STEPS)
            ]
            for first_tile in range(0, HALF // LANES, 2):
                chains = [
                    (tile, half) for tile in range(first_tile, first_tile + 2) for half in range(2)
                ]
                spans = [
                    slice(half * HALF + tile * LANES, half * HALF + (tile + 1) * LANES)
                    for tile, half in chains
                ]
                hidden = [state_ref[source, :, columns] for columns in spans]
                for step in range(STEPS):
                    first = (which * STEPS + step) * STATE
                    for index in range(len(chains)):
                        line = slice(which % 2 * STEPS + step, which % 2 * STEPS + step + 1)
                        speed = jnp.broadcast_to(rate[pair, line, spans[index]], (STATE, LANES))
                        feed = jnp.broadcast_to(fed[pair, line, spans[index]], (STATE, LANES))
                        hidden[index] = (
                            jnp.exp2(speed * decay[:, spans[index]]) * hidden[index]
                            + feed * into[step]
                        )
                        keep[first : first + STATE, spans[index]] = hidden[index].astype(BF16)

    def readout(quad, keep, acts):
        both = jnp.dot(read[quad], keep[...], preferred_element_type=F32)
        both = both[0:16] + both[16:32] + skip_ref[...] * acts
        for which in range(2):
            req = 4 * quad + 2 * which
            rows = slice(which * 8, which * 8 + 8)
            for tile in range(HALF // LANES):
                place = slice(tile * LANES, (tile + 1) * LANES)
                low = both[rows, place]
                high = both[rows, HALF + tile * LANES : HALF + (tile + 1) * LANES]
                even = jnp.where(upper, low, pltpu.roll(high, STEPS, 0))
                odd = jnp.where(upper, pltpu.roll(low, STEPS, 0), high)
                out_ref[req, :, place] = even.astype(BF16)
                out_ref[req + 1, :, place] = odd.astype(BF16)

    def some(index, carry):
        count = len(keeps)
        rows = pl.ds(pl.multiple_of(index * 16 * count, 16 * count), 16 * count)
        acts = act_ref[rows, :].astype(F32)
        for offset in range(count + 1):
            if offset < count:
                advance(count * index + offset, keeps[offset])
            if offset:
                last = offset - 1
                readout(count * index + last, keeps[last], acts[last * 16 : last * 16 + 16])
        return carry

    lax.fori_loop(0, REQS // 4 // len(keeps), some, 0)
    for req in range(REQS):
        out_ref[req, :, HALF:BACK] = attended_ref[req]


def scan(order, core, ours, theirs, act, attended, ssm_state, dt_proj, dt_bias, a_log, skip_d):
    return pl.pallas_call(
        scan_kernel,
        out_shape=jax.ShapeDtypeStruct((REQS, ROWS, BACK), BF16),
        in_specs=[smem(), smem()] + [vmem()] * 9,
        out_specs=vmem(),
        scratch_shapes=[
            pltpu.VMEM((REQS * STEPS, RANK + 2 * LANES), BF16),
            pltpu.VMEM((REQS // 2, ROWS, 2 * HALF), F32),
            pltpu.VMEM((REQS // 2, ROWS, 2 * HALF), F32),
            pltpu.VMEM((STATE, 2 * HALF), F32),
            pltpu.VMEM((LANES, LANES), F32),
            pltpu.VMEM((REQS // 4, 32, 2 * LANES), BF16),
        ]
        + [pltpu.VMEM((4 * STEPS * STATE, 2 * HALF), BF16)] * KEEPS,
        compiler_params=params(16),
        name="scan",
    )(order, core, ours, theirs, act, attended, ssm_state, dt_proj, dt_bias, a_log, skip_d)


def unpack_kernel(back_ref, z_ref, attn_hbm, mamba_hbm, rows, attn_ref, mamba_ref, sems):
    outs = []
    for group in range(0, REQS, 16):
        for req in range(group, group + 16):
            for tile in range(BACK // LANES):
                rows[tile, req * ROWS : (req + 1) * ROWS, :] = back_ref[
                    req, :, tile * LANES : (tile + 1) * LANES
                ].astype(F32)
        for step in range(STEPS):
            for half in range(2):
                first = half * STEPS + step
                places = [
                    pl.ds((group + part * 8) * ROWS + first, 8, stride=ROWS) for part in range(2)
                ]
                for tile in range(BACK // LANES):
                    block = jnp.concatenate([rows[tile, place, :] for place in places], axis=0)
                    if tile < HALF // LANES:
                        first_column = half * HALF + tile * LANES
                        columns = slice(first_column, first_column + LANES)
                        z = z_ref[step, group : group + 16, columns].astype(F32)
                        block = block * silu(z)
                        mamba_ref[step, group : group + 16, columns] = block.astype(BF16)
                    else:
                        first_column = half * QUARTER + tile * LANES - HALF
                        columns = slice(first_column, first_column + LANES)
                        attn_ref[step, group : group + 16, columns] = block.astype(BF16)
        span = pl.ds(group, 16)
        for index, (near, far) in enumerate(((attn_ref, attn_hbm), (mamba_ref, mamba_hbm))):
            outs.append(
                pltpu.make_async_copy(
                    near.at[:, span], far.at[:, span], sems.at[index, group // 16]
                )
            )
            outs[-1].start()
    for copy in outs:
        copy.wait()


def unpack(back, mamba_z):
    attn = (STEPS, REQS, 2 * QUARTER)
    mamba = (STEPS, REQS, 2 * HALF)
    return pl.pallas_call(
        unpack_kernel,
        out_shape=(jax.ShapeDtypeStruct(attn, BF16), jax.ShapeDtypeStruct(mamba, BF16)),
        in_specs=[vmem()] * 2,
        out_specs=(anywhere(), anywhere()),
        scratch_shapes=[
            pltpu.VMEM((BACK // LANES, REQS * ROWS, LANES), F32),
            pltpu.VMEM(attn, BF16),
            pltpu.VMEM(mamba, BF16),
            pltpu.SemaphoreType.DMA((2, 2)),
        ],
        compiler_params=params(24),
        name="unpack",
    )(back, mamba_z)


def per_device(
    queries,
    new_kv,
    prefill_page_pool,
    page_table,
    prompt_len,
    dest_device,
    ssm_state,
    conv_state,
    mamba_x,
    mamba_z,
    conv_weight,
    conv_bias,
    x_proj,
    dt_gain,
    dt_proj,
    dt_bias,
    a_log,
    skip_d,
):
    slots = jnp.arange(REQS, dtype=jnp.int32)
    order = jnp.sum(
        jnp.where(dest_device[None, :] == slots[:, None], slots[None, :], 0), axis=1
    )
    core = (lax.axis_index("tp") % 2).astype(jnp.int32).reshape(1)
    swap = [(j, j ^ 1) for j in range(8)]

    outgoing = pack(mamba_x, queries, new_kv)
    arrived = lax.all_to_all(outgoing, "req", split_axis=0, concat_axis=0, tiled=True)
    prior = stage(
        order, outgoing, jnp.transpose(conv_state, (1, 0, 2)), conv_weight, conv_bias[None]
    )
    act, mine, other = convolve(core, arrived, prior, x_proj)
    chip_sum = mine + lax.ppermute(other, "tp", swap)
    small = chip_sum.astype(BF16)
    ring = [
        lax.ppermute(small, "tp", [(j, (j + hop) % 8) for j in range(8)]) for hop in (4, 2, 6)
    ]
    attended = attend(order, page_table, prompt_len, arrived, prefill_page_pool)
    ours = normalise(chip_sum, ring, dt_gain[None], attended)
    theirs = lax.ppermute(ours, "tp", swap)
    returning = scan(
        order,
        core,
        ours,
        theirs,
        act,
        attended,
        ssm_state,
        dt_proj,
        dt_bias[None],
        a_log,
        skip_d[None],
    )
    back = lax.all_to_all(returning, "req", split_axis=0, concat_axis=0, tiled=True)
    return unpack(back, mamba_z)


def solution(mesh):
    return jax.shard_map(
        per_device,
        mesh=mesh,
        in_specs=(
            P(None, "req", "tp"),
            P(None, "req", None, "tp"),
            P("req", None, None, "tp"),
            P("req", None),
            P("req"),
            P("req"),
            P("req", None, "tp"),
            P("req", None, "tp"),
            P(None, "req", "tp"),
            P(None, "req", "tp"),
            P(None, "tp"),
            P("tp"),
            P("tp", None),
            P(),
            P(None, "tp"),
            P("tp"),
            P(None, "tp"),
            P("tp"),
        ),
        out_specs=(P(None, "req", "tp"), P(None, "req", "tp")),
        check_vma=False,
    )
```

```python
import math

import jax
import jax.numpy as jnp
from jax import lax
from jax.experimental import pallas as pl
from jax.experimental.pallas import tpu as pltpu
from jax.sharding import PartitionSpec as P

HEAD_SIZE = 128
EPSILON = 1e-06
REQS = 32
STEPS = 4
ROWS = 2 * STEPS
LANES = 128
HALF = 1024
QUARTER = 512
RANK = 512
STATE = 16
PAGES = 8
WHOLE = 63
BIG = 60
UNROLL = 32
KEEPS = 8
CHUNKS = 4
PAGE_TOKENS = 16
PROJ = RANK + 2 * STATE
SEND = HALF + QUARTER + HEAD_SIZE
BACK = HALF + QUARTER
F32 = jnp.float32
BF16 = jnp.bfloat16


def vmem():
    return pl.BlockSpec(memory_space=pltpu.VMEM)


def anywhere():
    return pl.BlockSpec(memory_space=pl.ANY)


def smem():
    return pl.BlockSpec(memory_space=pltpu.SMEM)


def params(mib):
    return pltpu.CompilerParams(vmem_limit_bytes=mib * 1024 * 1024)


def cost(mb):
    return pl.CostEstimate(
        flops=3_500_000_000, bytes_accessed=mb * 1_000_000, transcendentals=300_000
    )


def softplus(x):
    return jnp.maximum(x, 0.0) + jnp.log(1.0 + jnp.exp(-jnp.abs(x)))


def silu(x):
    half = 0.5 * x
    return half * jnp.tanh(half) + half


def sublanes(shape):
    return lax.broadcasted_iota(jnp.int32, shape, len(shape) - 2)


def pack_kernel(x_hbm, q_hbm, kv_hbm, out_hbm, x_ref, q_ref, kv_ref, rows, out_ref, sems, out_sems):
    groups = range(0, REQS, 16)
    copies = []
    for group in groups:
        span = pl.ds(group, 16)
        trio = ((x_hbm, x_ref), (q_hbm, q_ref), (kv_hbm, kv_ref))
        copies.append(
            [
                pltpu.make_async_copy(
                    far.at[:, span], near.at[:, span], sems.at[index, group // 16]
                )
                for index, (far, near) in enumerate(trio)
            ]
        )
        for copy in copies[-1]:
            copy.start()
    outs = []
    for group in groups:
        for copy in copies[group // 16]:
            copy.wait()
        for step in range(STEPS):
            for half in range(2):
                first = half * STEPS + step
                places = [
                    pl.ds((group + part * 8) * ROWS + first, 8, stride=ROWS) for part in range(2)
                ]
                tile = 0
                for ref, width in ((x_ref, HALF), (q_ref, QUARTER)):
                    block = ref[step, group : group + 16, half * width : (half + 1) * width]
                    block = block.astype(F32)
                    for column in range(0, width, LANES):
                        rows[tile, places[0], :] = block[0:8, column : column + LANES]
                        rows[tile, places[1], :] = block[8:16, column : column + LANES]
                        tile += 1
            for req in range(group, group + 16):
                rows[SEND // LANES - 1, pl.ds(req * ROWS + step, 2, stride=STEPS), :] = kv_ref[
                    step, req
                ].astype(F32)
        for req in range(group, group + 16):
            for tile in range(SEND // LANES):
                out_ref[req, :, tile * LANES : (tile + 1) * LANES] = rows[
                    tile, req * ROWS : (req + 1) * ROWS, :
                ].astype(BF16)
        span = pl.ds(group, 16)
        outs.append(
            pltpu.make_async_copy(out_ref.at[span], out_hbm.at[span], out_sems.at[group // 16])
        )
        outs[-1].start()
    for copy in outs:
        copy.wait()


def pack(mamba_x, queries, new_kv):
    return pl.pallas_call(
        pack_kernel,
        out_shape=jax.ShapeDtypeStruct((REQS, ROWS, SEND), BF16),
        in_specs=[anywhere()] * 3,
        out_specs=anywhere(),
        scratch_shapes=[
            pltpu.VMEM((STEPS, REQS, 2 * HALF), BF16),
            pltpu.VMEM((STEPS, REQS, 2 * QUARTER), BF16),
            pltpu.VMEM((STEPS, REQS, 2, HEAD_SIZE), BF16),
            pltpu.VMEM((SEND // LANES, REQS * ROWS, LANES), F32),
            pltpu.VMEM((REQS, ROWS, SEND), BF16),
            pltpu.SemaphoreType.DMA((3, 2)),
            pltpu.SemaphoreType.DMA((2,)),
        ],
        compiler_params=params(BIG),
        name="pack",
    )(mamba_x, queries, new_kv)


def halves(ref, row, width):
    low = jnp.broadcast_to(ref[row : row + 1, 0:width], (STEPS, width))
    high = jnp.broadcast_to(ref[row : row + 1, width : 2 * width], (STEPS, width))
    return jnp.concatenate([low, high], axis=0)


def stage_kernel(order_ref, sent_ref, past_ref, weight_ref, bias_ref, out_ref, past_rows, past_taps):
    del sent_ref
    step_of = lax.rem(sublanes((ROWS, HALF)), STEPS)
    for tap in range(3):
        for half in range(2):
            for tile in range(HALF // LANES):
                column = half * HALF + tile * LANES
                block = past_ref[tap, :, column : column + LANES].astype(F32)
                for group in range(0, REQS, 8):
                    place = pl.ds(group * ROWS + (1 - half) * STEPS + 1 + tap, 8, stride=ROWS)
                    past_rows[tile, place, :] = block[group : group + 8]
    plain = [halves(weight_ref, tap, HALF) for tap in range(4)]
    for back in range(4):
        out_ref[REQS + back] = jnp.where(step_of >= back, plain[3 - back], 0.0)
        past_taps[back] = plain[3 - back]
    past_taps[0] = halves(bias_ref, 0, HALF)

    def one(req, carry):
        first = pl.multiple_of(order_ref[req] * ROWS, ROWS)
        past = jnp.concatenate(
            [past_rows[tile, pl.ds(first, ROWS), :] for tile in range(HALF // LANES)], axis=1
        )
        total = past_taps[0]
        for back in range(1, 4):
            moved = jnp.where(step_of < back, pltpu.roll(past, back, 0), 0.0)
            total = total + past_taps[back] * moved
        out_ref[req] = total
        return carry

    lax.fori_loop(0, REQS, one, 0)


def stage(order, sent, conv_state, conv_weight, conv_bias):
    return pl.pallas_call(
        stage_kernel,
        out_shape=jax.ShapeDtypeStruct((REQS + 4, ROWS, HALF), F32),
        in_specs=[smem(), anywhere()] + [vmem()] * 3,
        out_specs=vmem(),
        scratch_shapes=[
            pltpu.VMEM((HALF // LANES, REQS * ROWS, LANES), F32),
            pltpu.VMEM((4, ROWS, HALF), F32),
        ],
        compiler_params=pltpu.CompilerParams(vmem_limit_bytes=(64 * 1024 - 600) * 1024),
        name="stage",
    )(order, sent, conv_state, conv_weight, conv_bias)


def conv_kernel(
    core_ref,
    rows_hbm,
    prior_hbm,
    proj_hbm,
    act_hbm,
    mine_ref,
    other_ref,
    rows_ref,
    prior_ref,
    proj_ref,
    act_ref,
    part,
    rows_sems,
    prior_sems,
    proj_sem,
    act_sem,
):
    chunk = REQS // CHUNKS
    arriving = [
        pltpu.make_async_copy(
            prior_hbm.at[pl.ds(REQS, 4)], prior_ref.at[pl.ds(REQS, 4)], prior_sems.at[CHUNKS]
        )
    ]
    for index in range(CHUNKS):
        span = pl.ds(index * chunk, chunk)
        arriving.append(
            pltpu.make_async_copy(
                rows_hbm.at[span, :, pl.ds(0, HALF)], rows_ref.at[span], rows_sems.at[index]
            )
        )
        arriving.append(
            pltpu.make_async_copy(prior_hbm.at[span], prior_ref.at[span], prior_sems.at[index])
        )
    proj_copy = pltpu.make_async_copy(proj_hbm, proj_ref, proj_sem)
    for copy in arriving + [proj_copy]:
        copy.start()
    arriving[0].wait()

    def one(req):
        now = rows_ref[req].astype(F32)
        total = prior_ref[req] + prior_ref[REQS] * now
        for back in range(1, 4):
            total = total + prior_ref[REQS + back] * pltpu.roll(now, back, 0)
        return silu(total)

    upper = sublanes((ROWS, HALF)) < STEPS

    def some(index, carry):
        lows, highs = [], []
        for offset in range(0, 4, 2):
            even, odd = one(4 * index + offset), one(4 * index + offset + 1)
            lows.append(jnp.where(upper, even, pltpu.roll(odd, STEPS, 0)))
            highs.append(jnp.where(upper, pltpu.roll(even, STEPS, 0), odd))
        rows = pl.ds(pl.multiple_of(index * 16, 16), 16)
        act_ref[rows, 0:HALF] = jnp.concatenate(lows, axis=0).astype(BF16)
        act_ref[rows, HALF:] = jnp.concatenate(highs, axis=0).astype(BF16)
        return carry

    for index in range(CHUNKS):
        arriving[1 + 2 * index].wait()
        arriving[2 + 2 * index].wait()
        lax.fori_loop(index * chunk // 4, (index + 1) * chunk // 4, some, 0)
    act_copy = pltpu.make_async_copy(act_ref, act_hbm, act_sem)
    act_copy.start()
    proj_copy.wait()
    part[...] = jnp.dot(act_ref[...], proj_ref[...], preferred_element_type=F32)
    core = core_ref[0]
    size = REQS * STEPS // 2
    mine_ref[...] = part[pl.ds(pl.multiple_of(core * size, size), size), :]
    other_ref[...] = part[pl.ds(pl.multiple_of((1 - core) * size, size), size), :]
    act_copy.wait()


def convolve(core, arrived, prior, x_proj):
    half_rows = jax.ShapeDtypeStruct((REQS * STEPS // 2, PROJ), F32)
    return pl.pallas_call(
        conv_kernel,
        out_shape=(jax.ShapeDtypeStruct((REQS * STEPS, 2 * HALF), BF16), half_rows, half_rows),
        in_specs=[smem()] + [anywhere()] * 3,
        out_specs=(anywhere(), vmem(), vmem()),
        scratch_shapes=[
            pltpu.VMEM((REQS, ROWS, HALF), BF16),
            pltpu.VMEM(prior.shape, F32),
            pltpu.VMEM(x_proj.shape, BF16),
            pltpu.VMEM((REQS * STEPS, 2 * HALF), BF16),
            pltpu.VMEM((REQS * STEPS, PROJ), F32),
            pltpu.SemaphoreType.DMA((CHUNKS,)),
            pltpu.SemaphoreType.DMA((CHUNKS + 1,)),
            pltpu.SemaphoreType.DMA,
            pltpu.SemaphoreType.DMA,
        ],
        compiler_params=params(52),
        name="convolve",
    )(core, arrived, prior, x_proj)


def norm_kernel(sum_ref, one_ref, two_ref, three_ref, gain_ref, after_ref, out_ref):
    del after_ref
    total = (
        sum_ref[...]
        + one_ref[...].astype(F32)
        + two_ref[...].astype(F32)
        + three_ref[...].astype(F32)
    )
    low = total[:, :RANK]
    spread = lax.rsqrt(jnp.mean(low * low, axis=-1, keepdims=True) + EPSILON)
    out_ref[:, 0:RANK] = (low * spread * gain_ref[...]).astype(BF16)
    coef = total[:, RANK:]
    coef = jnp.concatenate([coef, jnp.zeros((coef.shape[0], LANES - 2 * STATE), F32)], axis=1)
    coef_high = coef.astype(BF16)
    out_ref[:, RANK : RANK + LANES] = coef_high
    out_ref[:, RANK + LANES :] = (coef - coef_high.astype(F32)).astype(BF16)


def normalise(chip_sum, ring, gain, after):
    return pl.pallas_call(
        norm_kernel,
        out_shape=jax.ShapeDtypeStruct((REQS * STEPS // 2, RANK + 2 * LANES), BF16),
        in_specs=[vmem()] * 5 + [anywhere()],
        out_specs=vmem(),
        compiler_params=params(8),
        name="normalise",
    )(chip_sum, *ring, gain, after)


def attend_kernel(
    order_ref, table_ref, length_ref, rows_ref, pool_ref, out_ref, scores_ref, weights_ref
):
    scale = math.log2(math.e) / math.sqrt(HEAD_SIZE)
    count = 4 * ROWS
    lane = lax.broadcasted_iota(jnp.int32, (count, LANES), 1)
    step_of = lax.rem(lax.broadcasted_iota(jnp.int32, (count, LANES), 0), STEPS)
    fresh_ok = lane <= step_of
    pad = jnp.zeros((LANES - PAGE_TOKENS, HEAD_SIZE), BF16)
    blank = jnp.zeros((ROWS, HEAD_SIZE), F32)
    ones = jnp.ones((2 * LANES, LANES), BF16)

    def score(req):
        source = order_ref[req]
        query = rows_ref[req, :, HALF : HALF + QUARTER].astype(F32)
        query = jnp.concatenate(
            [query[:, h * HEAD_SIZE : (h + 1) * HEAD_SIZE] for h in range(4)], axis=0
        ).astype(BF16)
        fresh = rows_ref[req, :, HALF + QUARTER : SEND].astype(F32)
        fresh = jnp.concatenate([fresh, blank], axis=0).astype(BF16)
        keys = [pool_ref[table_ref[source, page], 0] for page in range(PAGES)]
        keys = jnp.concatenate(keys + [fresh, pad], axis=0)
        scores_ref[req] = lax.dot_general(
            query, keys, (((1,), (1,)), ((), ())), preferred_element_type=F32
        )

    def soften(req):
        length = length_ref[order_ref[req]]
        old = jnp.where(lane < length, scores_ref[req, :, 0:LANES] * scale, -jnp.inf)
        new = jnp.where(fresh_ok, scores_ref[req, :, LANES:] * scale, -jnp.inf)
        top = jnp.max(jnp.maximum(old, new), axis=1, keepdims=True)
        weights_ref[req, :, 0:LANES] = jnp.exp2(old - top).astype(BF16)
        weights_ref[req, :, LANES:] = jnp.exp2(new - top).astype(BF16)

    def mix(req):
        source = order_ref[req]
        fresh = rows_ref[req, :, HALF + QUARTER : SEND].astype(F32)
        fresh = jnp.concatenate([pltpu.roll(fresh, STEPS, 0), blank], axis=0).astype(BF16)
        values = [pool_ref[table_ref[source, page], 1] for page in range(PAGES)]
        values = jnp.concatenate(values + [fresh, pad], axis=0)
        values = jnp.concatenate([values, ones], axis=1)
        mixed = jnp.dot(weights_ref[req], values, preferred_element_type=F32)
        mixed = mixed[:, 0:LANES] / mixed[:, LANES:]
        for h in range(4):
            out_ref[req, :, h * HEAD_SIZE : (h + 1) * HEAD_SIZE] = mixed[
                h * ROWS : (h + 1) * ROWS
            ].astype(BF16)

    for phase in (score, soften, mix):

        def some(index, carry, phase=phase):
            for offset in range(UNROLL):
                phase(UNROLL * index + offset)
            return carry

        lax.fori_loop(0, REQS // UNROLL, some, 0)


def attend(order, page_table, prompt_len, arrived, pool):
    return pl.pallas_call(
        attend_kernel,
        out_shape=jax.ShapeDtypeStruct((REQS, ROWS, QUARTER), BF16),
        in_specs=[smem()] * 3 + [vmem()] * 2,
        out_specs=vmem(),
        scratch_shapes=[
            pltpu.VMEM((REQS, 4 * ROWS, 2 * LANES), F32),
            pltpu.VMEM((REQS, 4 * ROWS, 2 * LANES), BF16),
        ],
        compiler_params=params(8),
        cost_estimate=cost(6),
        name="attend",
    )(order, page_table, prompt_len, arrived, pool)


def scan_kernel(
    order_ref,
    core_ref,
    ours_ref,
    theirs_ref,
    act_ref,
    attended_ref,
    state_ref,
    dt_proj_ref,
    dt_bias_ref,
    a_log_ref,
    skip_ref,
    out_ref,
    packed,
    rate,
    fed,
    decay,
    coef,
    read,
    *keeps,
):
    core = core_ref[0]
    size = REQS * STEPS // 2
    packed[pl.ds(pl.multiple_of(core * size, size), size), :] = ours_ref[...]
    packed[pl.ds(pl.multiple_of((1 - core) * size, size), size), :] = theirs_ref[...]
    decay[...] = jnp.exp(a_log_ref[...]) * (-1.0 / math.log(2.0))
    coef[...] = jnp.transpose(
        packed[:, RANK : RANK + LANES].astype(F32) + packed[:, RANK + LANES :].astype(F32)
    )
    speeds = jnp.dot(packed[:, 0:RANK], dt_proj_ref[...], preferred_element_type=F32)
    speeds = softplus(speeds + dt_bias_ref[...])
    feeds = speeds * act_ref[...].astype(F32)
    for pair in range(REQS // 2):
        rows = slice(pair * 8, pair * 8 + 8)
        rate[pair] = speeds[rows]
        fed[pair] = feeds[rows]
    lane = lax.broadcasted_iota(jnp.int32, (REQS * STEPS, LANES), 1)
    row = lax.broadcasted_iota(jnp.int32, (REQS * STEPS, LANES), 0)
    parts = []
    for first in (RANK, RANK + LANES):
        part = packed[:, first : first + LANES].astype(F32)
        spread = jnp.zeros_like(part)
        for block in range(LANES // STATE):
            moved = pltpu.roll(part, (block * STATE - STATE) % LANES, 1)
            spread = jnp.where(
                (lane // STATE == block) & (lax.rem(row, 2 * STEPS) == block), moved, spread
            )
        parts.append(spread)
    first_pair = lax.rem(row, 4 * STEPS) < 2 * STEPS
    for quad in range(REQS // 4):
        rows = slice(quad * 16, quad * 16 + 16)
        for side in range(2):
            block = [jnp.where(first_pair == (side == 0), part, 0.0)[rows] for part in parts]
            read[quad, :, side * LANES : (side + 1) * LANES] = jnp.concatenate(
                block, axis=0
            ).astype(BF16)
    upper = sublanes((ROWS, LANES)) < STEPS

    def advance(quad, keep):
        for which in range(4):
            req = 4 * quad + which
            pair = 2 * quad + which // 2
            source = order_ref[req]
            turned = pltpu.roll(coef[0:STATE, :], lax.rem(LANES - STEPS * req, LANES), 1)
            into = [
                jnp.broadcast_to(turned[:, s : s + 1], (STATE, LANES)) for s in range(STEPS)
            ]
            for first_tile in range(0, HALF // LANES, 2):
                chains = [
                    (tile, half) for tile in range(first_tile, first_tile + 2) for half in range(2)
                ]
                spans = [
                    slice(half * HALF + tile * LANES, half * HALF + (tile + 1) * LANES)
                    for tile, half in chains
                ]
                hidden = [state_ref[source, :, columns] for columns in spans]
                for step in range(STEPS):
                    first = (which * STEPS + step) * STATE
                    for index in range(len(chains)):
                        line = slice(which % 2 * STEPS + step, which % 2 * STEPS + step + 1)
                        speed = jnp.broadcast_to(rate[pair, line, spans[index]], (STATE, LANES))
                        feed = jnp.broadcast_to(fed[pair, line, spans[index]], (STATE, LANES))
                        hidden[index] = (
                            jnp.exp2(speed * decay[:, spans[index]]) * hidden[index]
                            + feed * into[step]
                        )
                        keep[first : first + STATE, spans[index]] = hidden[index].astype(BF16)

    def readout(quad, keep, acts):
        both = jnp.dot(read[quad], keep[...], preferred_element_type=F32)
        both = both[0:16] + both[16:32] + skip_ref[...] * acts
        for which in range(2):
            req = 4 * quad + 2 * which
            rows = slice(which * 8, which * 8 + 8)
            for tile in range(HALF // LANES):
                place = slice(tile * LANES, (tile + 1) * LANES)
                low = both[rows, place]
                high = both[rows, HALF + tile * LANES : HALF + (tile + 1) * LANES]
                even = jnp.where(upper, low, pltpu.roll(high, STEPS, 0))
                odd = jnp.where(upper, pltpu.roll(low, STEPS, 0), high)
                out_ref[req, :, place] = even.astype(BF16)
                out_ref[req + 1, :, place] = odd.astype(BF16)

    def some(index, carry):
        count = len(keeps)
        rows = pl.ds(pl.multiple_of(index * 16 * count, 16 * count), 16 * count)
        acts = act_ref[rows, :].astype(F32)
        for offset in range(count + 1):
            if offset < count:
                advance(count * index + offset, keeps[offset])
            if offset:
                last = offset - 1
                readout(count * index + last, keeps[last], acts[last * 16 : last * 16 + 16])
        return carry

    lax.fori_loop(0, REQS // 4 // len(keeps), some, 0)
    for req in range(REQS):
        out_ref[req, :, HALF:BACK] = attended_ref[req]


def scan(order, core, ours, theirs, act, attended, ssm_state, dt_proj, dt_bias, a_log, skip_d):
    return pl.pallas_call(
        scan_kernel,
        out_shape=jax.ShapeDtypeStruct((REQS, ROWS, BACK), BF16),
        in_specs=[smem(), smem()] + [vmem()] * 9,
        out_specs=vmem(),
        scratch_shapes=[
            pltpu.VMEM((REQS * STEPS, RANK + 2 * LANES), BF16),
            pltpu.VMEM((REQS // 2, ROWS, 2 * HALF), F32),
            pltpu.VMEM((REQS // 2, ROWS, 2 * HALF), F32),
            pltpu.VMEM((STATE, 2 * HALF), F32),
            pltpu.VMEM((LANES, LANES), F32),
            pltpu.VMEM((REQS // 4, 32, 2 * LANES), BF16),
        ]
        + [pltpu.VMEM((4 * STEPS * STATE, 2 * HALF), BF16)] * KEEPS,
        compiler_params=params(40),
        name="scan",
    )(order, core, ours, theirs, act, attended, ssm_state, dt_proj, dt_bias, a_log, skip_d)


def unpack_kernel(back_ref, z_ref, attn_hbm, mamba_hbm, rows, attn_ref, mamba_ref, sems):
    outs = []
    for group in range(0, REQS, 16):
        for req in range(group, group + 16):
            for tile in range(BACK // LANES):
                rows[tile, req * ROWS : (req + 1) * ROWS, :] = back_ref[
                    req, :, tile * LANES : (tile + 1) * LANES
                ].astype(F32)
        for step in range(STEPS):
            for half in range(2):
                first = half * STEPS + step
                places = [
                    pl.ds((group + part * 8) * ROWS + first, 8, stride=ROWS) for part in range(2)
                ]
                for tile in range(BACK // LANES):
                    block = jnp.concatenate([rows[tile, place, :] for place in places], axis=0)
                    if tile < HALF // LANES:
                        first_column = half * HALF + tile * LANES
                        columns = slice(first_column, first_column + LANES)
                        z = z_ref[step, group : group + 16, columns].astype(F32)
                        block = block * silu(z)
                        mamba_ref[step, group : group + 16, columns] = block.astype(BF16)
                    else:
                        first_column = half * QUARTER + tile * LANES - HALF
                        columns = slice(first_column, first_column + LANES)
                        attn_ref[step, group : group + 16, columns] = block.astype(BF16)
        span = pl.ds(group, 16)
        for index, (near, far) in enumerate(((attn_ref, attn_hbm), (mamba_ref, mamba_hbm))):
            outs.append(
                pltpu.make_async_copy(
                    near.at[:, span], far.at[:, span], sems.at[index, group // 16]
                )
            )
            outs[-1].start()
    for copy in outs:
        copy.wait()


def unpack(back, mamba_z):
    attn = (STEPS, REQS, 2 * QUARTER)
    mamba = (STEPS, REQS, 2 * HALF)
    return pl.pallas_call(
        unpack_kernel,
        out_shape=(jax.ShapeDtypeStruct(attn, BF16), jax.ShapeDtypeStruct(mamba, BF16)),
        in_specs=[vmem()] * 2,
        out_specs=(anywhere(), anywhere()),
        scratch_shapes=[
            pltpu.VMEM((BACK // LANES, REQS * ROWS, LANES), F32),
            pltpu.VMEM(attn, BF16),
            pltpu.VMEM(mamba, BF16),
            pltpu.SemaphoreType.DMA((2, 2)),
        ],
        compiler_params=params(24),
        name="unpack",
    )(back, mamba_z)


def per_device(
    queries,
    new_kv,
    prefill_page_pool,
    page_table,
    prompt_len,
    dest_device,
    ssm_state,
    conv_state,
    mamba_x,
    mamba_z,
    conv_weight,
    conv_bias,
    x_proj,
    dt_gain,
    dt_proj,
    dt_bias,
    a_log,
    skip_d,
):
    slots = jnp.arange(REQS, dtype=jnp.int32)
    order = jnp.sum(
        jnp.where(dest_device[None, :] == slots[:, None], slots[None, :], 0), axis=1
    )
    core = (lax.axis_index("tp") % 2).astype(jnp.int32).reshape(1)
    swap = [(j, j ^ 1) for j in range(8)]

    outgoing = pack(mamba_x, queries, new_kv)
    arrived = lax.all_to_all(outgoing, "req", split_axis=0, concat_axis=0, tiled=True)
    prior = stage(
        order, outgoing, jnp.transpose(conv_state, (1, 0, 2)), conv_weight, conv_bias[None]
    )
    act, mine, other = convolve(core, arrived, prior, x_proj)
    chip_sum = mine + lax.ppermute(other, "tp", swap)
    small = chip_sum.astype(BF16)
    ring = [
        lax.ppermute(small, "tp", [(j, (j + hop) % 8) for j in range(8)]) for hop in (4, 2, 6)
    ]
    attended = attend(order, page_table, prompt_len, arrived, prefill_page_pool)
    ours = normalise(chip_sum, ring, dt_gain[None], attended)
    theirs = lax.ppermute(ours, "tp", swap)
    returning = scan(
        order,
        core,
        ours,
        theirs,
        act,
        attended,
        ssm_state,
        dt_proj,
        dt_bias[None],
        a_log,
        skip_d[None],
    )
    back = lax.all_to_all(returning, "req", split_axis=0, concat_axis=0, tiled=True)
    return unpack(back, mamba_z)


def solution(mesh):
    return jax.shard_map(
        per_device,
        mesh=mesh,
        in_specs=(
            P(None, "req", "tp"),
            P(None, "req", None, "tp"),
            P("req", None, None, "tp"),
            P("req", None),
            P("req"),
            P("req"),
            P("req", None, "tp"),
            P("req", None, "tp"),
            P(None, "req", "tp"),
            P(None, "req", "tp"),
            P(None, "tp"),
            P("tp"),
            P("tp", None),
            P(),
            P(None, "tp"),
            P("tp"),
            P(None, "tp"),
            P("tp"),
        ),
        out_specs=(P(None, "req", "tp"), P(None, "req", "tp")),
        check_vma=False,
    )
```
